512 devices in a mesh: gz: 64 (over z, x, y_lo), gy: 8 (over y_hi, core).
Axes of the slice: x: 4, y: 8 (y_hi: 4, y_lo: 2; y = y_hi * 2 + y_lo), z: 8, core: 2. Of those that a mesh axis runs over, the one named last changes fastest.
Arguments:
- observed: float32 [512, 128, 1024], P('gz', 'gy'), may hold values from 0.2 to 5
- estimate: float32 [512, 128, 1024], P('gz', 'gy'), may hold values from 0.5 to 2
- psf_y: float32 [31], replicated, may hold values from 0.05 to 1
- psf_x: float32 [31], replicated, may hold values from 0.05 to 1
- psf_z: float32 [63], replicated, may hold values from 0.05 to 1
Outputs:
- restored: float32 [512, 128, 1024], P('gz', 'gy')
The draws below stay inside these ranges and needn't reach their ends.
All inputs are finite; a program needn't handle non-finite values.
Results may differ from the reference program's by a relative error of at most 0.0001.
Values sent between devices are 32-bit elements; how exact they have to be, the bound alone decides.
No kernel may reach another device: no remote copies, remote signals or barrier semaphores. Data moves between devices by JAX's collectives and lax.ppermute only.
A program may use at most 64 MiB of HBM per device.

```python
import math
import jax
import jax.numpy as jnp
from jax import lax

NX = 1024
KY = 31
KX = 31
KZ = 63
ITERS = 2
NZ = 512
NY = 128


def block_levels(key, dims, split, least, high):
    def one(axis_at, blocks):
        heights = jax.random.uniform(jax.random.fold_in(jax.random.fold_in(key, 6), axis_at), (blocks,), jnp.float32, least / len(split), high / len(split))
        return jnp.repeat(jnp.exp(heights), dims[axis_at] // blocks).reshape((-1,) + (1,) * (len(dims) - axis_at - 1))

    level = one(*split[0])
    for cut in split[1:]:
        level = level * one(*cut)
    return level


def setup_inputs(seed: int = 0) -> dict:
    arg_keys = jax.random.split(jax.random.key(seed), 6)
    return {
        "observed": jnp.clip(jnp.exp(math.log(5.0) - 3.218876 * jax.random.uniform(arg_keys[0], (NZ, NY, NX), jnp.float32) ** block_levels(arg_keys[0], (NZ, NY, NX), ((0, 64), (1, 8)), -0.2, 0.2)), 0.2, 5.0),
        "estimate": jnp.clip(jnp.exp(math.log(2.0) - 1.3862944 * jax.random.uniform(arg_keys[1], (NZ, NY, NX), jnp.float32) ** block_levels(arg_keys[1], (NZ, NY, NX), ((0, 64), (1, 8)), -0.2, 0.2)), 0.5, 2.0),
        "psf_y": jnp.clip(jnp.exp(jax.random.uniform(arg_keys[2], (KY,), jnp.float32, math.log(0.05), math.log(1.0))), 0.05, 1.0),
        "psf_x": jnp.clip(jnp.exp(jax.random.uniform(arg_keys[3], (KX,), jnp.float32, math.log(0.05), math.log(1.0))), 0.05, 1.0),
        "psf_z": jnp.clip(jnp.exp(jax.random.uniform(arg_keys[4], (KZ,), jnp.float32, math.log(0.05), math.log(1.0))), 0.05, 1.0),
    }


def blur_along(volume, weights, along_axis):
    length = volume.shape[along_axis]
    width = weights.shape[0]
    reach = width // 2
    padded_len = length + width - 1
    spectrum = jnp.fft.rfft(volume, n=padded_len, axis=along_axis)
    target_shape = [1, 1, 1]
    target_shape[along_axis] = padded_len // 2 + 1
    kernel = jnp.fft.rfft(weights, n=padded_len).reshape(target_shape)
    convolved = jnp.fft.irfft(spectrum * kernel, n=padded_len, axis=along_axis)
    return lax.slice_in_dim(convolved, reach, reach + length, axis=along_axis).astype(volume.dtype)


def reference(observed, estimate, psf_y, psf_x, psf_z):
    wy = psf_y / jnp.sum(psf_y)
    wx = psf_x / jnp.sum(psf_x)
    wz = psf_z / jnp.sum(psf_z)
    for sweep in range(ITERS):
        blurred = blur_along(blur_along(blur_along(estimate, wy[::-1], 1), wx[::-1], 2), wz[::-1], 0)
        ratio = observed / blurred
        back = blur_along(blur_along(blur_along(ratio, wz, 0), wy, 1), wx, 2)
        estimate = estimate * back
    return estimate
```

```python
import jax
import jax.numpy as jnp
import numpy as np
from jax import lax
from jax.sharding import Mesh, PartitionSpec as P

ITERS = 2
HI = lax.Precision.HIGHEST
SLAB = ("x", "yl", "yh", "c")


def toeplitz(w, rows, cols, lead):
    taps = w.shape[0]
    period = cols + rows
    line = jnp.pad(w, (lead, period + 1 - lead - taps))
    flat = jnp.tile(line, rows)[: rows * period]
    return flat.reshape(rows, period)[:, :cols]


def x_index(b, c):
    x, yh, yl = b // 8, (b % 8) // 2, b % 2
    return ((x * 2 + yl) * 4 + yh) * 2 + c


SWAP = [(0, 1), (1, 0)]
NEXT = [(x_index(b, 0), x_index(b - 1, 1)) for b in range(1, 32)] + [
    (x_index(b, 1), x_index(b + 1, 0)) for b in range(31)
]
Z_FWD = [(((z + 1) % 8) * 2, z * 2) for z in range(8)] + [
    (((z - 1) % 8) * 2 + 1, z * 2 + 1) for z in range(8)
]
Z_ADJ = [(d, s) for s, d in Z_FWD]


def enter(volume):
    t = volume.reshape(128, 1024).T.reshape(4, 4, 2, 2, 16, 128)
    t = t.transpose(0, 2, 1, 3, 4, 5).reshape(64, 16, 128)
    t = lax.all_to_all(t, SLAB, 0, 0, tiled=True)
    t = t.reshape(8, 8, 16, 8, 16).transpose(2, 0, 3, 1, 4)
    return t.reshape(16, 64, 128)


def leave(block):
    t = block.reshape(16, 8, 8, 8, 16).transpose(1, 3, 0, 2, 4).reshape(64, 16, 128)
    t = lax.all_to_all(t, SLAB, 0, 0, tiled=True)
    t = t.reshape(4, 2, 4, 2, 16, 128).transpose(0, 2, 1, 3, 4, 5).reshape(1024, 128)
    return t.T.reshape(8, 16, 1024)


def per_device(observed, estimate, psf_y, psf_x, psf_z):
    core = lax.axis_index("c")
    slab = lax.axis_index("z")
    first = core == 0
    wy = psf_y / jnp.sum(psf_y)
    wx = psf_x / jnp.sum(psf_x)
    wz = psf_z / jnp.sum(psf_z)

    est = enter(estimate)
    obs = enter(observed)

    own_half = jnp.where(first, obs[:, :32], obs[:, 32:])
    keep = jnp.where(first, obs[:, 32:], obs[:, :32])
    got = lax.ppermute(own_half, ("z", "c"), Z_FWD)
    obs = jnp.concatenate([jnp.where(first, keep, got), jnp.where(first, got, keep)], axis=1)

    y_fwd = toeplitz(jnp.pad(wy, (0, 0)), 128, 158, 0)[:, 15:143].T
    y_adj = toeplitz(wy[::-1], 128, 158, 0)[:, 15:143].T

    row = lax.broadcasted_iota(jnp.int32, (64, 64), 0)
    col = lax.broadcasted_iota(jnp.int32, (64, 64), 1)
    zf = toeplitz(wz, 64, 128, 1)
    za = toeplitz(wz[::-1], 64, 128, 1)
    seam = jnp.where(first, slab == 7, slab == 0)
    f_lo = jnp.where(seam & (row >= 32), 0, zf[:, :64])
    f_hi = jnp.where(seam & (row < 32), 0, zf[:, 64:])
    a_lo = jnp.where((slab == 0) & (col < 32), 0, za[:, :64])
    a_hi = jnp.where((slab == 7) & (col >= 32), 0, za[:, 64:])
    f_own, f_got = jnp.where(first, f_lo, f_hi), jnp.where(first, f_hi, f_lo)
    a_own, a_got = jnp.where(first, a_hi, a_lo), jnp.where(first, a_lo, a_hi)

    def y_blur(v, m):
        return jnp.einsum("xzq,qy->xzy", v, m, precision=HI)

    def x_blur(v, w):
        swapped = lax.ppermute(v, "c", SWAP)
        passed = lax.ppermute(v, SLAB, NEXT)
        low = jnp.where(first, passed, swapped)
        high = jnp.where(first, swapped, passed)
        ext = jnp.concatenate([low, v, high], axis=0)
        total = w[0] * ext[1:17]
        for k in range(1, 31):
            total = total + w[k] * ext[k + 1 : k + 17]
        return total

    def z_blur(v, own, other, perm):
        got = lax.ppermute(v, ("z", "c"), perm)
        return jnp.einsum("xjy,ij->xiy", v, own, precision=HI) + jnp.einsum(
            "xjy,ij->xiy", got, other, precision=HI
        )

    for sweep in range(ITERS):
        blurred = z_blur(x_blur(y_blur(est, y_fwd), wx), f_own, f_got, Z_FWD)
        ratio = obs / blurred
        back = y_blur(x_blur(z_blur(ratio, a_own, a_got, Z_ADJ), wx[::-1]), y_adj)
        est = est * back
    return leave(est)


def solution(mesh):
    fine = Mesh(mesh.devices.reshape(8, 4, 2, 4, 2), ("z", "x", "yl", "yh", "c"))
    spec = P(("z", "x", "yl"), ("yh", "c"), None)
    return jax.shard_map(
        per_device,
        mesh=fine,
        in_specs=(spec, spec, P(), P(), P()),
        out_specs=spec,
        check_vma=False,
    )
```

```python
import functools

import jax
import jax.numpy as jnp
from jax import lax
from jax.experimental import pallas as pl
from jax.experimental.pallas import tpu as pltpu
from jax.sharding import Mesh, PartitionSpec as P

ITERS = 2
HI = lax.Precision.HIGHEST
SLAB = ("x", "yl", "yh", "c")
BLOCK = jax.ShapeDtypeStruct((16, 64, 128), jnp.float32)
VMEM = pl.BlockSpec(memory_space=pltpu.VMEM)
SMEM = pl.BlockSpec(memory_space=pltpu.SMEM)


def x_index(b, c):
    x, yh, yl = b // 8, (b % 8) // 2, b % 2
    return ((x * 2 + yl) * 4 + yh) * 2 + c


SWAP = [(0, 1), (1, 0)]
NEXT = [(x_index(b, 0), x_index(b - 1, 1)) for b in range(1, 32)] + [
    (x_index(b, 1), x_index(b + 1, 0)) for b in range(31)
]
Z_FWD = [(((z + 1) % 8) * 2, z * 2) for z in range(8)] + [
    (((z - 1) % 8) * 2 + 1, z * 2 + 1) for z in range(8)
]
Z_ADJ = [(d, s) for s, d in Z_FWD]


def cost(us):
    return pl.CostEstimate(flops=int(us * 1e6), bytes_accessed=int(us * 3e6), transcendentals=0)


def swap_groups(tile):
    row = lax.broadcasted_iota(jnp.int32, (8, 128), 0)
    group = lax.broadcasted_iota(jnp.int32, (8, 128), 1) // 16
    for b in (1, 2, 4):
        up = pltpu.roll(pltpu.roll(tile, 8 - b, 0), 16 * b, 1)
        down = up if b == 4 else pltpu.roll(pltpu.roll(tile, b, 0), 128 - 16 * b, 1)
        take_up = ((row & b) == 0) & ((group & b) != 0)
        take_down = ((row & b) != 0) & ((group & b) == 0)
        tile = jnp.where(take_up, up, jnp.where(take_down, down, tile))
    return tile


def unpack_kernel(in_ref, out_ref):
    for zc in range(8):
        for x in range(16):
            tile = in_ref[pl.ds(zc * 128 + x, 8, stride=16), :]
            out_ref[x, zc * 8 : zc * 8 + 8, :] = swap_groups(tile)


def pack_kernel(in_ref, out_ref):
    for zc in range(8):
        for x in range(16):
            tile = in_ref[x, zc * 8 : zc * 8 + 8, :]
            out_ref[pl.ds(zc * 128 + x, 8, stride=16), :] = swap_groups(tile)


def unpack(rows):
    return pl.pallas_call(
        unpack_kernel, out_shape=BLOCK, in_specs=[VMEM], out_specs=VMEM, cost_estimate=cost(1), name="unpack"
    )(rows)


def pack(block):
    return pl.pallas_call(
        pack_kernel,
        out_shape=jax.ShapeDtypeStruct((1024, 128), jnp.float32),
        in_specs=[VMEM],
        out_specs=VMEM,
        cost_estimate=cost(1),
        name="pack",
    )(block)


def enter(volume):
    t = volume.reshape(128, 1024).T.reshape(4, 4, 2, 2, 16, 128)
    t = t.transpose(0, 2, 1, 3, 4, 5).reshape(64, 16, 128)
    t = lax.all_to_all(t, SLAB, 0, 0, tiled=True)
    return unpack(t.reshape(1024, 128))


def leave(block):
    t = pack(block).reshape(64, 16, 128)
    t = lax.all_to_all(t, SLAB, 0, 0, tiled=True)
    t = t.reshape(4, 2, 4, 2, 16, 128).transpose(0, 2, 1, 3, 4, 5).reshape(1024, 128)
    return t.T.reshape(8, 16, 1024)


def tap_vectors(psf_ref, flip):
    total = psf_ref[0]
    for k in range(1, 31):
        total = total + psf_ref[k]
    scale = 1.0 / jnp.full((8, 128), total, jnp.float32)
    return [psf_ref[30 - k if flip else k] * scale for k in range(31)]


def x_own_kernel(flip, psf_ref, own_ref, out_ref):
    w = tap_vectors(psf_ref, flip)

    def body(t, _):
        z = pl.ds(pl.multiple_of(t * 8, 8), 8)
        acc = [None] * 16
        for j in range(16):
            v = own_ref[j, z, :]
            for i in range(16):
                p = w[j - i + 15] * v
                acc[i] = p if acc[i] is None else acc[i] + p
        for i in range(16):
            out_ref[i, z, :] = acc[i]
        return 0

    lax.fori_loop(0, 8, body, 0)


def x_rest_kernel(flip, psf_ref, core_ref, part_ref, passed_ref, swapped_ref, out_ref):
    w = tap_vectors(psf_ref, flip)

    def run(low_ref, high_ref):
        def body(t, _):
            z = pl.ds(pl.multiple_of(t * 8, 8), 8)
            acc = [part_ref[i, z, :] for i in range(16)]
            for j in range(16):
                low, high = low_ref[j, z, :], high_ref[j, z, :]
                for i in range(16):
                    if i < j:
                        acc[i] = acc[i] + w[j - i - 1] * low
                    if i > j:
                        acc[i] = acc[i] + w[j - i + 31] * high
            for i in range(16):
                out_ref[i, z, :] = acc[i]
            return 0

        lax.fori_loop(0, 8, body, 0)

    @pl.when(core_ref[0] == 0)
    def _():
        run(passed_ref, swapped_ref)

    @pl.when(core_ref[0] != 0)
    def _():
        run(swapped_ref, passed_ref)


def x_blur(v, psf, core, flip):
    swapped = lax.ppermute(v, "c", SWAP)
    passed = lax.ppermute(v, SLAB, NEXT)
    part = pl.pallas_call(
        functools.partial(x_own_kernel, flip),
        out_shape=BLOCK,
        in_specs=[SMEM, VMEM],
        out_specs=VMEM,
        cost_estimate=cost(1),
        name="x_own",
    )(psf, v)
    return pl.pallas_call(
        functools.partial(x_rest_kernel, flip),
        out_shape=BLOCK,
        in_specs=[SMEM, SMEM, VMEM, VMEM, VMEM],
        out_specs=VMEM,
        cost_estimate=cost(1),
        name="x_rest",
    )(psf, core, part, passed, swapped)


def prep_kernel(place_ref, lines_ref, yf_ref, ya_ref, fo_ref, fg_ref, ao_ref, ag_ref):
    slab, first = place_ref[0], place_ref[1] == 0

    def band(at, rows):
        line = lines_ref[at : at + 1, :]
        line = line / jnp.sum(line, axis=1, keepdims=True)
        return pltpu.roll(jnp.broadcast_to(line, (rows, 256)), 0, 1, stride=1, stride_axis=0)

    yf_ref[...] = band(0, 128)[:, :128]
    ya_ref[...] = band(1, 128)[:, :128]
    row = lax.broadcasted_iota(jnp.int32, (64, 128), 0)
    col = lax.broadcasted_iota(jnp.int32, (64, 128), 1)
    fwd, adj = band(2, 64)[:, :128], band(3, 64)[:, :128]
    seam = (first & (slab == 7)) | (jnp.logical_not(first) & (slab == 0))
    seam = jnp.where(seam, 1, 0)
    fwd = jnp.where((seam == 1) & ((row >= 32) == (col < 64)), 0.0, fwd)
    bottom, top = jnp.where(slab == 0, 1, 0), jnp.where(slab == 7, 1, 0)
    adj = jnp.where((bottom == 1) & (col < 32), 0.0, adj)
    adj = jnp.where((top == 1) & (col >= 96), 0.0, adj)
    fl, fh, al, ah = fwd[:, :64], fwd[:, 64:], adj[:, :64], adj[:, 64:]
    pick = jnp.where(first, 1, 0) == 1
    fo_ref[...] = jnp.where(pick, fl, fh)
    fg_ref[...] = jnp.where(pick, fh, fl)
    ao_ref[...] = jnp.where(pick, ah, al)
    ag_ref[...] = jnp.where(pick, al, ah)


def prepare(psf_y, psf_z, slab, core):
    def line(taps, start):
        return jnp.roll(jnp.pad(taps, (0, 256 - taps.shape[0])), start)

    lines = jnp.stack(
        [line(psf_y[::-1], -15), line(psf_y, -15), line(psf_z, 1), line(psf_z[::-1], 1)]
    )
    lines = jnp.concatenate([lines, lines], axis=0)
    square = jax.ShapeDtypeStruct((128, 128), jnp.float32)
    small = jax.ShapeDtypeStruct((64, 64), jnp.float32)
    return pl.pallas_call(
        prep_kernel,
        out_shape=[square, square, small, small, small, small],
        in_specs=[SMEM, VMEM],
        out_specs=[VMEM] * 6,
        cost_estimate=cost(2),
        name="prepare",
    )(jnp.stack([slab, core]), lines)


def y_blur(v, m):
    return jnp.einsum("xzq,qy->xzy", v, m, precision=HI)


def z_blur(v, own, other, perm):
    got = lax.ppermute(v, ("z", "c"), perm)
    near = jnp.einsum("xjy,ij->xiy", v, own, precision=HI)
    return near + jnp.einsum("xjy,ij->xiy", got, other, precision=HI)


def per_device(observed, estimate, psf_y, psf_x, psf_z):
    core = lax.axis_index("c")
    slab = lax.axis_index("z")
    first = core == 0
    core_at = core.reshape(1)
    y_fwd, y_adj, f_own, f_got, a_own, a_got = prepare(psf_y, psf_z, slab, core)

    est = enter(estimate)
    obs = enter(observed)

    send = jnp.where(first, obs[:, :32], obs[:, 32:])
    keep = jnp.where(first, obs[:, 32:], obs[:, :32])
    got = lax.ppermute(send, ("z", "c"), Z_FWD)
    obs = jnp.concatenate([jnp.where(first, keep, got), jnp.where(first, got, keep)], axis=1)

    for sweep in range(ITERS):
        blurred = x_blur(y_blur(est, y_fwd), psf_x, core_at, False)
        ratio = obs / z_blur(blurred, f_own, f_got, Z_FWD)
        back = x_blur(z_blur(ratio, a_own, a_got, Z_ADJ), psf_x, core_at, True)
        est = est * y_blur(back, y_adj)
    return leave(est)


def solution(mesh):
    fine = Mesh(mesh.devices.reshape(8, 4, 2, 4, 2), ("z", "x", "yl", "yh", "c"))
    spec = P(("z", "x", "yl"), ("yh", "c"), None)
    return jax.shard_map(
        per_device,
        mesh=fine,
        in_specs=(spec, spec, P(), P(), P()),
        out_specs=spec,
        check_vma=False,
    )
```

```python
import functools

import jax
import jax.numpy as jnp
from jax import lax
from jax.experimental import pallas as pl
from jax.experimental.pallas import tpu as pltpu
from jax.sharding import Mesh, PartitionSpec as P

ITERS = 2
HI = lax.Precision.HIGHEST
SLAB = ("x", "yl", "yh", "c")
BLOCK = (16, 64, 128)
VMEM = pl.BlockSpec(memory_space=pltpu.VMEM)
SMEM = pl.BlockSpec(memory_space=pltpu.SMEM)


def x_index(b, c):
    x, yh, yl = b // 8, (b % 8) // 2, b % 2
    return ((x * 2 + yl) * 4 + yh) * 2 + c


SWAP = [(0, 1), (1, 0)]
NEXT = [(x_index(b, 0), x_index(b - 1, 1)) for b in range(1, 32)] + [
    (x_index(b, 1), x_index(b + 1, 0)) for b in range(31)
]
Z_FWD = [(((z + 1) % 8) * 2, z * 2) for z in range(8)] + [
    (((z - 1) % 8) * 2 + 1, z * 2 + 1) for z in range(8)
]
Z_ADJ = [(d, s) for s, d in Z_FWD]


def cost(us):
    return pl.CostEstimate(flops=int(us * 1e6), bytes_accessed=int(us * 3e6), transcendentals=0)


def swap_groups(tiles):
    group = lax.broadcasted_iota(jnp.int32, (8, 128), 1) // 16
    tiles = [tiles[0]] + [pltpu.roll(tiles[i], 16 * i, 1) for i in range(1, 8)]
    for b in (1, 2, 4):
        taken = (group & b) != 0
        tiles = [jnp.where(taken, tiles[(i + b) % 8], tiles[i]) for i in range(8)]
    return [tiles[0]] + [pltpu.roll(tiles[8 - i], 128 - 16 * i, 1) for i in range(1, 8)]


def unpack_kernel(in_ref, out_ref, rows_ref):
    for zc in range(8):
        for half in range(2):
            at = zc * 128 + half * 8
            tiles = swap_groups([in_ref[at + 16 * i : at + 16 * i + 8, :] for i in range(8)])
            for i in range(8):
                rows_ref[at + 16 * i : at + 16 * i + 8, :] = tiles[i]
    for zc in range(8):
        for x in range(16):
            out_ref[x, zc * 8 : zc * 8 + 8, :] = rows_ref[pl.ds(zc * 128 + x, 8, stride=16), :]


def pack_kernel(in_ref, out_ref, rows_ref):
    for zc in range(8):
        for x in range(16):
            rows_ref[pl.ds(zc * 128 + x, 8, stride=16), :] = in_ref[x, zc * 8 : zc * 8 + 8, :]
    for zc in range(8):
        for half in range(2):
            at = zc * 128 + half * 8
            tiles = swap_groups([rows_ref[at + 16 * i : at + 16 * i + 8, :] for i in range(8)])
            for i in range(8):
                out_ref[at + 16 * i : at + 16 * i + 8, :] = tiles[i]


def call(kernel, out, args, us, name, scratch=()):
    pinned = [a if a.ndim == 1 else pltpu.with_memory_space_constraint(a, pltpu.VMEM) for a in args]
    return pl.pallas_call(
        kernel,
        out_shape=jax.tree.map(lambda s: pltpu.VMEM(s, jnp.float32), out, is_leaf=lambda s: isinstance(s, tuple)),
        in_specs=[SMEM if a.ndim == 1 else VMEM for a in args],
        out_specs=jax.tree.map(lambda s: VMEM, out, is_leaf=lambda s: isinstance(s, tuple)),
        scratch_shapes=[pltpu.VMEM(s, jnp.float32) for s in scratch],
        cost_estimate=cost(us),
        name=name,
    )(*pinned)


def unpack(rows):
    return call(unpack_kernel, BLOCK, [rows], 1, "unpack", [(1024, 128)])


def pack(block):
    return call(pack_kernel, (1024, 128), [block], 1, "pack", [(1024, 128)])


def enter(volume):
    t = volume.reshape(128, 1024).T.reshape(4, 4, 2, 2, 16, 128)
    t = t.transpose(0, 2, 1, 3, 4, 5).reshape(64, 16, 128)
    t = lax.all_to_all(t, SLAB, 0, 0, tiled=True)
    return unpack(t.reshape(1024, 128))


def leave(block):
    t = pack(block).reshape(64, 16, 128)
    t = lax.all_to_all(t, SLAB, 0, 0, tiled=True)
    t = t.reshape(4, 2, 4, 2, 16, 128).transpose(0, 2, 1, 3, 4, 5).reshape(1024, 128)
    return t.T.reshape(8, 16, 1024)


def tap_vectors(psf_ref, flip):
    total = psf_ref[0]
    for k in range(1, 31):
        total = total + psf_ref[k]
    scale = 1.0 / jnp.full((8, 128), total, jnp.float32)
    return [psf_ref[30 - k if flip else k] * scale for k in range(31)]


def x_own_kernel(flip, psf_ref, own_ref, out_ref):
    w = tap_vectors(psf_ref, flip)

    def body(t, _):
        z = pl.ds(pl.multiple_of(t * 8, 8), 8)
        acc = [None] * 16
        for j in range(16):
            v = own_ref[j, z, :]
            for i in range(16):
                p = w[j - i + 15] * v
                acc[i] = p if acc[i] is None else acc[i] + p
        for i in range(16):
            out_ref[i, z, :] = acc[i]
        return 0

    lax.fori_loop(0, 8, body, 0)


def x_rest_kernel(flip, psf_ref, core_ref, part_ref, passed_ref, swapped_ref, out_ref):
    w = tap_vectors(psf_ref, flip)

    def run(low_ref, high_ref):
        def body(t, _):
            z = pl.ds(pl.multiple_of(t * 8, 8), 8)
            acc = [part_ref[i, z, :] for i in range(16)]
            for j in range(16):
                low, high = low_ref[j, z, :], high_ref[j, z, :]
                for i in range(16):
                    if i < j:
                        acc[i] = acc[i] + w[j - i - 1] * low
                    if i > j:
                        acc[i] = acc[i] + w[j - i + 31] * high
            for i in range(16):
                out_ref[i, z, :] = acc[i]
            return 0

        lax.fori_loop(0, 8, body, 0)

    @pl.when(core_ref[0] == 0)
    def _():
        run(passed_ref, swapped_ref)

    @pl.when(core_ref[0] != 0)
    def _():
        run(swapped_ref, passed_ref)


def x_blur(v, psf, core, flip):
    swapped = lax.ppermute(v, "c", SWAP)
    passed = lax.ppermute(v, SLAB, NEXT)
    part = call(functools.partial(x_own_kernel, flip), BLOCK, [psf, v], 1.3, "x_own")
    return call(
        functools.partial(x_rest_kernel, flip), BLOCK, [psf, core, part, passed, swapped], 1.3, "x_rest"
    )


def prep_kernel(place_ref, lines_ref, yf_ref, ya_ref, fo_ref, fg_ref, ao_ref, ag_ref):
    slab, first = place_ref[0], place_ref[1] == 0

    def band(at, rows):
        line = lines_ref[at : at + 1, :]
        line = line / jnp.sum(line, axis=1, keepdims=True)
        return pltpu.roll(jnp.broadcast_to(line, (rows, 256)), 0, 1, stride=1, stride_axis=0)

    yf_ref[...] = band(0, 128)[:, :128]
    ya_ref[...] = band(1, 128)[:, :128]
    row = lax.broadcasted_iota(jnp.int32, (64, 128), 0)
    col = lax.broadcasted_iota(jnp.int32, (64, 128), 1)
    fwd, adj = band(2, 64)[:, :128], band(3, 64)[:, :128]
    seam = (first & (slab == 7)) | (jnp.logical_not(first) & (slab == 0))
    seam = jnp.where(seam, 1, 0)
    fwd = jnp.where((seam == 1) & ((row >= 32) == (col < 64)), 0.0, fwd)
    bottom, top = jnp.where(slab == 0, 1, 0), jnp.where(slab == 7, 1, 0)
    adj = jnp.where((bottom == 1) & (col < 32), 0.0, adj)
    adj = jnp.where((top == 1) & (col >= 96), 0.0, adj)
    fl, fh, al, ah = fwd[:, :64], fwd[:, 64:], adj[:, :64], adj[:, 64:]
    pick = jnp.where(first, 1, 0) == 1
    fo_ref[...] = jnp.where(pick, fl, fh)
    fg_ref[...] = jnp.where(pick, fh, fl)
    ao_ref[...] = jnp.where(pick, ah, al)
    ag_ref[...] = jnp.where(pick, al, ah)


def prepare(psf_y, psf_z, slab, core):
    def line(taps, start):
        return jnp.roll(jnp.pad(taps, (0, 256 - taps.shape[0])), start)

    lines = jnp.stack(
        [line(psf_y[::-1], -15), line(psf_y, -15), line(psf_z, 1), line(psf_z[::-1], 1)]
    )
    lines = jnp.concatenate([lines, lines], axis=0)
    out = [(128, 128)] * 2 + [(64, 64)] * 4
    return call(prep_kernel, out, [jnp.stack([slab, core]), lines], 2, "prepare")


def y_blur(v, m):
    return jnp.einsum("xzq,qy->xzy", v, m, precision=HI)


def z_blur(v, own, other, perm):
    got = lax.ppermute(v, ("z", "c"), perm)
    near = jnp.einsum("xjy,ij->xiy", v, own, precision=HI)
    return near + jnp.einsum("xjy,ij->xiy", got, other, precision=HI)


def per_device(observed, estimate, psf_y, psf_x, psf_z):
    core = lax.axis_index("c")
    slab = lax.axis_index("z")
    first = core == 0
    core_at = core.reshape(1)
    y_fwd, y_adj, f_own, f_got, a_own, a_got = prepare(psf_y, psf_z, slab, core)

    est = enter(estimate)
    obs = enter(observed)

    send = jnp.where(first, obs[:, :32], obs[:, 32:])
    keep = jnp.where(first, obs[:, 32:], obs[:, :32])
    got = lax.ppermute(send, ("z", "c"), Z_FWD)
    obs = jnp.concatenate([jnp.where(first, keep, got), jnp.where(first, got, keep)], axis=1)

    for sweep in range(ITERS):
        blurred = x_blur(y_blur(est, y_fwd), psf_x, core_at, False)
        ratio = obs / z_blur(blurred, f_own, f_got, Z_FWD)
        back = x_blur(z_blur(ratio, a_own, a_got, Z_ADJ), psf_x, core_at, True)
        est = est * y_blur(back, y_adj)
    return leave(est)


def solution(mesh):
    fine = Mesh(mesh.devices.reshape(8, 4, 2, 4, 2), ("z", "x", "yl", "yh", "c"))
    spec = P(("z", "x", "yl"), ("yh", "c"), None)
    return jax.shard_map(
        per_device,
        mesh=fine,
        in_specs=(spec, spec, P(), P(), P()),
        out_specs=spec,
        check_vma=False,
    )
```

```python
import functools

import jax
import jax.numpy as jnp
from jax import lax
from jax.experimental import pallas as pl
from jax.experimental.pallas import tpu as pltpu
from jax.sharding import Mesh, PartitionSpec as P

HI = lax.Precision.HIGHEST
SLAB = ("x", "yl", "yh", "c")
BLOCK = (16, 64, 128)
ROWS = (1024, 128)
VMEM = pl.BlockSpec(memory_space=pltpu.VMEM)
SMEM = pl.BlockSpec(memory_space=pltpu.SMEM)


def x_index(b, c):
    x, yh, yl = b // 8, (b % 8) // 2, b % 2
    return ((x * 2 + yl) * 4 + yh) * 2 + c


SWAP = [(0, 1), (1, 0)]
NEXT = [(x_index(b, 0), x_index(b - 1, 1)) for b in range(1, 32)] + [
    (x_index(b, 1), x_index(b + 1, 0)) for b in range(31)
]
UP = [(z, z + 1) for z in range(7)]
DOWN = [(z + 1, z) for z in range(7)]


def is_shape(s):
    return isinstance(s, tuple)


def call(kernel, out, args, us, name, scratch=()):
    pinned = [a if a.ndim == 1 else pltpu.with_memory_space_constraint(a, pltpu.VMEM) for a in args]
    return pl.pallas_call(
        kernel,
        out_shape=jax.tree.map(lambda s: pltpu.VMEM(s, jnp.float32), out, is_leaf=is_shape),
        in_specs=[SMEM if a.ndim == 1 else VMEM for a in args],
        out_specs=jax.tree.map(lambda s: VMEM, out, is_leaf=is_shape),
        scratch_shapes=[pltpu.VMEM(s, jnp.float32) for s in scratch],
        cost_estimate=pl.CostEstimate(
            flops=int(us * 1e6), bytes_accessed=int(us * 3e6), transcendentals=0
        ),
        compiler_params=pltpu.CompilerParams(vmem_limit_bytes=16 * 2**20),
        name=name,
    )(*pinned)


def dot(a, b):
    return jnp.dot(a, b, precision=HI, preferred_element_type=jnp.float32)


def band(psf_ref, lead, flip, rows):
    taps = psf_ref.shape[0]
    lane = lax.broadcasted_iota(jnp.int32, (8, 256), 1)
    line = jnp.zeros((8, 256), jnp.float32)
    total = psf_ref[0]
    for k in range(taps):
        if k:
            total = total + psf_ref[k]
        line = jnp.where(lane == (k + lead) % 256, psf_ref[taps - 1 - k if flip else k], line)
    line = line / jnp.full((8, 256), total, jnp.float32)
    return pltpu.roll(jnp.broadcast_to(line[:1], (rows, 256)), 0, 1, stride=1, stride_axis=0)


def x_band(psf_ref, flip):
    m = band(psf_ref, -15, not flip, 128)
    return m[:, :128], m[:, 128:]


def prep_kernel(psf_y_ref, psf_z_ref, yf_ref, ya_ref, zo_ref, zl_ref, zh_ref, za_ref):
    yf_ref[...] = band(psf_y_ref, -15, True, 128)[:, :128]
    ya_ref[...] = band(psf_y_ref, -15, False, 128)[:, :128]
    fwd = band(psf_z_ref, 1, False, 128)
    zl_ref[...] = fwd[:64, :64]
    zo_ref[...] = fwd[:, 64:128]
    zh_ref[...] = fwd[64:, 128:192]
    za_ref[...] = band(psf_z_ref, 1, True, 64)[:, :128]


def prepare(psf_y, psf_z):
    out = [(128, 128), (128, 128), (128, 64), (64, 64), (64, 64), (64, 128)]
    return call(prep_kernel, out, [psf_y, psf_z], 1, "prepare")


def blur_lanes(tiles, near, far):
    lane = lax.broadcasted_iota(jnp.int32, tiles[0].shape, 1)
    zero = jnp.zeros_like(tiles[0])
    out = []
    for t in range(8):
        after = tiles[t + 1] if t < 7 else zero
        before = tiles[t - 1] if t > 0 else zero
        out.append(dot(tiles[t], near) + dot(jnp.where(lane < 64, after, before), far))
    return out


def rows_at(t, i, per=16, offset=0):
    block = 8 * t + i
    return x_index(block // 2, block % 2) * per + offset


def write_columns(out_ref, t, tile, per=16, offset=0):
    turned = tile.T
    for i in range(8):
        at = rows_at(t, i, per, offset)
        out_ref[at : at + 16, :] = turned[16 * i : 16 * i + 16, :]


def first_kernel(psf_x_ref, est_ref, obs_ref, out_ref):
    near, far = x_band(psf_x_ref, False)
    blurred = blur_lanes([est_ref[:, 128 * t : 128 * t + 128] for t in range(8)], near, far)
    for t in range(8):
        write_columns(out_ref, t, blurred[t], 32, 0)
        write_columns(out_ref, t, obs_ref[:, 128 * t : 128 * t + 128], 32, 16)


def turn_kernel(in_ref, out_ref):
    for t in range(8):
        write_columns(out_ref, t, in_ref[:, 128 * t : 128 * t + 128])


def last_kernel(psf_x_ref, back_ref, est_ref, out_ref):
    near, far = x_band(psf_x_ref, True)

    def tile(ref, t):
        spots = [rows_at(t, i) for i in range(8)]
        return jnp.concatenate([ref[at : at + 16, :] for at in spots], axis=0).T

    blurred = blur_lanes([tile(back_ref, t) for t in range(8)], near, far)
    for t in range(8):
        out_ref[:, 128 * t : 128 * t + 128] = blurred[t] * tile(est_ref, t)


def swap_groups(tiles):
    group = lax.broadcasted_iota(jnp.int32, (8, 128), 1) // 16
    tiles = [tiles[0]] + [pltpu.roll(tiles[i], 16 * i, 1) for i in range(1, 8)]
    for b in (1, 2, 4):
        taken = (group & b) != 0
        tiles = [jnp.where(taken, tiles[(i + b) % 8], tiles[i]) for i in range(8)]
    return [tiles[0]] + [pltpu.roll(tiles[8 - i], 128 - 16 * i, 1) for i in range(1, 8)]


def unpack_one(in_ref, out_ref, rows_ref, per, offset):
    for zc in range(8):
        for half in range(2):
            at = zc * 8 * per + half * 8 + offset
            tiles = swap_groups([in_ref[at + per * i : at + per * i + 8, :] for i in range(8)])
            at = zc * 128 + half * 8
            for i in range(8):
                rows_ref[at + 16 * i : at + 16 * i + 8, :] = tiles[i]
    for zc in range(8):
        for x in range(16):
            out_ref[x, zc * 8 : zc * 8 + 8, :] = rows_ref[pl.ds(zc * 128 + x, 8, stride=16), :]


def unpack_kernel(in_ref, out_ref, rows_ref):
    unpack_one(in_ref, out_ref, rows_ref, 16, 0)


def unpack_pair_kernel(in_ref, y_ref, a_ref, b_ref, rows_ref, more_ref):
    unpack_one(in_ref, a_ref, rows_ref, 32, 0)
    for x in range(16):
        a_ref[x] = dot(a_ref[x], y_ref[...])
    unpack_one(in_ref, b_ref, more_ref, 32, 16)


def pack_kernel(in_ref, out_ref, rows_ref):
    for zc in range(8):
        for x in range(16):
            rows_ref[pl.ds(zc * 128 + x, 8, stride=16), :] = in_ref[x, zc * 8 : zc * 8 + 8, :]
    for zc in range(8):
        for half in range(2):
            at = zc * 128 + half * 8
            tiles = swap_groups([rows_ref[at + 16 * i : at + 16 * i + 8, :] for i in range(8)])
            for i in range(8):
                out_ref[at + 16 * i : at + 16 * i + 8, :] = tiles[i]


def exchange(rows):
    per = rows.shape[0] // 64
    t = lax.all_to_all(rows.reshape(64, per, 128), SLAB, 0, 0, tiled=True)
    return t.reshape(rows.shape)


def tap_vectors(psf_ref, flip):
    total = psf_ref[0]
    for k in range(1, 31):
        total = total + psf_ref[k]
    scale = 1.0 / jnp.full((8, 128), total, jnp.float32)
    return [psf_ref[30 - k if flip else k] * scale for k in range(31)]


def add_block(w, ref, z, acc, shift):
    for j in range(16):
        v = ref[j, z, :]
        for i in range(16):
            k = j + shift - i + 15
            if 0 <= k <= 30:
                p = w[k] * v
                acc[i] = p if acc[i] is None else acc[i] + p
    return acc


def over_planes(body):
    def step(t, _):
        body(pl.ds(pl.multiple_of(t * 8, 8), 8))
        return 0

    lax.fori_loop(0, 8, step, 0)


def near_kernel(flip, psf_ref, core_ref, own_ref, swapped_ref, out_ref):
    w = tap_vectors(psf_ref, flip)

    def run(shift):
        def body(z):
            acc = add_block(w, own_ref, z, [None] * 16, 0)
            acc = add_block(w, swapped_ref, z, acc, shift)
            for i in range(16):
                out_ref[i, z, :] = acc[i]

        over_planes(body)

    pl.when(core_ref[0] == 0)(lambda: run(16))
    pl.when(core_ref[0] != 0)(lambda: run(-16))


def far_part(w, core_ref, part_ref, passed_ref, finish):
    def run(shift):
        def body(z):
            acc = [part_ref[i, z, :] for i in range(16)]
            finish(z, add_block(w, passed_ref, z, acc, shift))

        over_planes(body)

    pl.when(core_ref[0] == 0)(lambda: run(-16))
    pl.when(core_ref[0] != 0)(lambda: run(16))


def far_kernel(flip, psf_ref, core_ref, part_ref, passed_ref, out_ref):
    w = tap_vectors(psf_ref, flip)

    def finish(z, acc):
        for i in range(16):
            out_ref[i, z, :] = acc[i]

    far_part(w, core_ref, part_ref, passed_ref, finish)


def update_kernel(flip, psf_ref, core_ref, part_ref, passed_ref, est_ref, y_ref, new_ref, out_ref):
    w = tap_vectors(psf_ref, flip)

    def finish(z, acc):
        for i in range(16):
            new_ref[i, z, :] = est_ref[i, z, :] * acc[i]

    far_part(w, core_ref, part_ref, passed_ref, finish)
    for i in range(16):
        out_ref[i] = dot(new_ref[i], y_ref[...])


def x_halo(v, psf, core, flip):
    passed = lax.ppermute(v, SLAB, NEXT)
    swapped = lax.ppermute(v, "c", SWAP)
    near = call(functools.partial(near_kernel, flip), BLOCK, [psf, core, v, swapped], 2, "x_near")
    return near, passed


def own_kernel(v_ref, zo_ref, out_ref):
    for x in range(16):
        out_ref[x] = dot(zo_ref[...], v_ref[x])


def ratio_kernel(
    slab_ref, part_ref, below_ref, above_ref, obs_ref, obs_below_ref, obs_above_ref,
    zl_ref, zh_ref, za_ref, ya_ref, out_ref, ratio_ref
):
    has_below = jnp.full((32, 128), slab_ref[0], jnp.int32) > 0
    has_above = jnp.full((32, 128), slab_ref[0], jnp.int32) < 7
    for x in range(16):
        low = part_ref[x, :64, :] + dot(zl_ref[...], below_ref[x])
        high = part_ref[x, 64:, :] + dot(zh_ref[...], above_ref[x])
        ratio_ref[x, :32, :] = jnp.where(has_below, obs_below_ref[x] / low[:32], 0.0)
        ratio_ref[x, 32:64, :] = obs_ref[x, :32, :] / low[32:]
        ratio_ref[x, 64:96, :] = obs_ref[x, 32:, :] / high[:32]
        ratio_ref[x, 96:, :] = jnp.where(has_above, obs_above_ref[x] / high[32:], 0.0)
    for x in range(16):
        out_ref[x] = dot(dot(za_ref[...], ratio_ref[x]), ya_ref[...])


def per_device(observed, estimate, psf_y, psf_x, psf_z):
    core = lax.axis_index("c").reshape(1)
    slab = lax.axis_index("z").reshape(1)
    est0 = estimate.reshape(128, 1024)

    first = call(first_kernel, (2048, 128), [psf_x, est0, observed.reshape(128, 1024)], 4, "first")
    arrived = exchange(first)
    yf, ya, zo, zl, zh, za = prepare(psf_y, psf_z)
    turned = call(turn_kernel, ROWS, [est0], 1, "turn")

    def z_phase(v, obs, obs_below, obs_above, riding):
        below = lax.ppermute(v, "z", UP)
        above = lax.ppermute(v, "z", DOWN)
        if obs_below is None:
            obs_below = lax.ppermute(obs[:, 32:], "z", UP)
            obs_above = lax.ppermute(obs[:, :32], "z", DOWN)
        part = call(own_kernel, (16, 128, 128), [v, zo], 1, "z_own")
        riding, part = lax.optimization_barrier((riding, part))
        rode = exchange(riding)
        back = call(
            ratio_kernel,
            BLOCK,
            [slab, part, below, above, obs, obs_below, obs_above, zl, zh, za, ya],
            4,
            "ratio",
            [(16, 128, 128)],
        )
        return back, rode, obs_below, obs_above

    v, obs = call(unpack_pair_kernel, [BLOCK, BLOCK], [arrived, yf], 2, "unpack_pair", [ROWS, ROWS])
    back, rode, obs_below, obs_above = z_phase(v, obs, None, None, turned)
    est = call(unpack_kernel, BLOCK, [rode], 1, "unpack", [ROWS])

    near, passed = x_halo(back, psf_x, core, True)
    est, v = call(
        functools.partial(update_kernel, True),
        [BLOCK, BLOCK],
        [psf_x, core, near, passed, est, yf],
        2,
        "update",
    )
    est_rows = call(pack_kernel, ROWS, [est], 1, "pack_est", [ROWS])
    near, passed = x_halo(v, psf_x, core, False)
    v = call(functools.partial(far_kernel, False), BLOCK, [psf_x, core, near, passed], 1, "x_far")

    back, rode, _, _ = z_phase(v, obs, obs_below, obs_above, est_rows)
    back = exchange(call(pack_kernel, ROWS, [back], 1, "pack_back", [ROWS]))
    out = call(last_kernel, (128, 1024), [psf_x, back, rode], 4, "last")
    return out.reshape(8, 16, 1024)


def solution(mesh):
    fine = Mesh(mesh.devices.reshape(8, 4, 2, 4, 2), ("z", "x", "yl", "yh", "c"))
    spec = P(("z", "x", "yl"), ("yh", "c"), None)
    return jax.shard_map(
        per_device,
        mesh=fine,
        in_specs=(spec, spec, P(), P(), P()),
        out_specs=spec,
        check_vma=False,
    )
```

```python
import functools

import jax
import jax.numpy as jnp
from jax import lax
from jax.experimental import pallas as pl
from jax.experimental.pallas import tpu as pltpu
from jax.sharding import Mesh, PartitionSpec as P

LIMIT = 6 * 2**20
SLAB = ("x", "yl", "yh", "c")
BLOCK = (16, 64, 128)
ROWS = (1024, 128)
VMEM = pl.BlockSpec(memory_space=pltpu.VMEM)
SMEM = pl.BlockSpec(memory_space=pltpu.SMEM)
HBM = pl.BlockSpec(memory_space=pltpu.HBM)


def x_index(b, c):
    x, yh, yl = b // 8, (b % 8) // 2, b % 2
    return ((x * 2 + yl) * 4 + yh) * 2 + c


SWAP = [(0, 1), (1, 0)]
NEXT = [(x_index(b, 0), x_index(b - 1, 1)) for b in range(1, 32)] + [
    (x_index(b, 1), x_index(b + 1, 0)) for b in range(31)
]
UP = [(z, z + 1) for z in range(7)]
DOWN = [(z + 1, z) for z in range(7)]


def is_shape(s):
    return isinstance(s, tuple)


def call(kernel, out, args, us, name, scratch=(), free=(), free_out=False):
    pinned = [
        a if a.ndim == 1 or i in free else pltpu.with_memory_space_constraint(a, pltpu.VMEM)
        for i, a in enumerate(args)
    ]
    kind = jax.ShapeDtypeStruct if free_out else pltpu.VMEM
    return pl.pallas_call(
        kernel,
        out_shape=jax.tree.map(lambda s: kind(s, jnp.float32), out, is_leaf=is_shape),
        in_specs=[SMEM if a.ndim == 1 else VMEM for a in args],
        out_specs=jax.tree.map(lambda s: VMEM, out, is_leaf=is_shape),
        scratch_shapes=[pltpu.VMEM(s, jnp.float32) for s in scratch],
        cost_estimate=pl.CostEstimate(
            flops=int(us * 1e9), bytes_accessed=int(us * 3e6), transcendentals=0
        ),
        compiler_params=pltpu.CompilerParams(vmem_limit_bytes=LIMIT),
        name=name,
    )(*pinned)


def split(m):
    high = m.astype(jnp.bfloat16)
    return high, (m - high.astype(jnp.float32)).astype(jnp.bfloat16)


def dot(a, b):
    (ah, al), (bh, bl) = a, b

    def one(p, q):
        return jnp.dot(p, q, preferred_element_type=jnp.float32)

    return one(ah, bh) + (one(al, bh) + one(ah, bl))


def band(psf_ref, lead, flip, rows):
    taps = psf_ref.shape[0]
    lane = lax.broadcasted_iota(jnp.int32, (8, 256), 1)
    line = jnp.zeros((8, 256), jnp.float32)
    total = psf_ref[0]
    for k in range(taps):
        if k:
            total = total + psf_ref[k]
        line = jnp.where(lane == (k + lead) % 256, psf_ref[taps - 1 - k if flip else k], line)
    line = line / jnp.full((8, 256), total, jnp.float32)
    return pltpu.roll(jnp.broadcast_to(line[:1], (rows, 256)), 0, 1, stride=1, stride_axis=0)


def x_band(psf_ref, flip):
    m = band(psf_ref, -15, not flip, 128)
    return m[:, :128], m[:, 128:]


def prep_kernel(psf_y_ref, psf_z_ref, yf_ref, ya_ref, zo_ref, zl_ref, zh_ref, za_ref):
    yf_ref[...] = band(psf_y_ref, -15, True, 128)[:, :128]
    ya_ref[...] = band(psf_y_ref, -15, False, 128)[:, :128]
    fwd = band(psf_z_ref, 1, False, 128)
    zl_ref[...] = fwd[:64, :64]
    zo_ref[...] = fwd[:, 64:128]
    zh_ref[...] = fwd[64:, 128:192]
    za_ref[...] = band(psf_z_ref, 1, True, 64)[:, :128]


def prepare(psf_y, psf_z):
    out = [(128, 128), (128, 128), (128, 64), (64, 64), (64, 64), (64, 128)]
    return call(prep_kernel, out, [psf_y, psf_z], 1, "prepare")


def blur_lanes(tiles, near, far):
    lane = lax.broadcasted_iota(jnp.int32, tiles[0].shape, 1)
    zero = jnp.zeros_like(tiles[0])
    near, far = split(near), split(far)
    out = []
    for t in range(8):
        after = tiles[t + 1] if t < 7 else zero
        before = tiles[t - 1] if t > 0 else zero
        out.append(dot(split(tiles[t]), near) + dot(split(jnp.where(lane < 64, after, before)), far))
    return out


def rows_at(t, i, per=16, offset=0):
    block = 8 * t + i
    return x_index(block // 2, block % 2) * per + offset


def write_columns(out_ref, t, tile, per=16, offset=0):
    turned = tile.T
    for i in range(8):
        at = rows_at(t, i, per, offset)
        out_ref[at : at + 16, :] = turned[16 * i : 16 * i + 16, :]


def first_kernel(psf_x_ref, est_hbm, obs_hbm, out_ref, est_ref, obs_ref, sems):
    copies = [
        pltpu.make_async_copy(
            src.at[pl.ds(16 * i, 16), :], dst.at[pl.ds(16 * i, 16), :], sems.at[8 * n + i]
        )
        for n, (src, dst) in enumerate(((est_hbm, est_ref), (obs_hbm, obs_ref)))
        for i in range(8)
    ]
    for copy in copies:
        copy.start()
    near, far = x_band(psf_x_ref, False)
    for copy in copies[:8]:
        copy.wait()
    blurred = blur_lanes([est_ref[:, 128 * t : 128 * t + 128] for t in range(8)], near, far)
    for t in range(8):
        write_columns(out_ref, t, blurred[t], 32, 0)
    for copy in copies[8:]:
        copy.wait()
    for t in range(8):
        write_columns(out_ref, t, obs_ref[:, 128 * t : 128 * t + 128], 32, 16)


def turn_kernel(in_ref, out_ref):
    for t in range(8):
        write_columns(out_ref, t, in_ref[:, 128 * t : 128 * t + 128])


def last_kernel(psf_x_ref, back_ref, est_ref, out_ref):
    near, far = x_band(psf_x_ref, True)

    def tile(ref, t):
        spots = [rows_at(t, i) for i in range(8)]
        return jnp.concatenate([ref[at : at + 16, :] for at in spots], axis=0).T

    blurred = blur_lanes([tile(back_ref, t) for t in range(8)], near, far)
    for t in range(8):
        out_ref[:, 128 * t : 128 * t + 128] = blurred[t] * tile(est_ref, t)


def swap_groups(tiles):
    group = lax.broadcasted_iota(jnp.int32, (8, 128), 1) // 16
    tiles = [tiles[0]] + [pltpu.roll(tiles[i], 16 * i, 1) for i in range(1, 8)]
    for b in (1, 2, 4):
        taken = (group & b) != 0
        tiles = [jnp.where(taken, tiles[(i + b) % 8], tiles[i]) for i in range(8)]
    return [tiles[0]] + [pltpu.roll(tiles[8 - i], 128 - 16 * i, 1) for i in range(1, 8)]


def unpack_one(in_ref, out_ref, rows_ref, per, offset):
    for zc in range(8):
        for half in range(2):
            at = zc * 8 * per + half * 8 + offset
            tiles = swap_groups([in_ref[at + per * i : at + per * i + 8, :] for i in range(8)])
            at = zc * 128 + half * 8
            for i in range(8):
                rows_ref[at + 16 * i : at + 16 * i + 8, :] = tiles[i]
    for zc in range(8):
        for x in range(16):
            out_ref[x, zc * 8 : zc * 8 + 8, :] = rows_ref[pl.ds(zc * 128 + x, 8, stride=16), :]


def unpack_kernel(in_ref, out_ref, rows_ref):
    unpack_one(in_ref, out_ref, rows_ref, 16, 0)


def arrive_kernel(in_ref, y_ref, up_ref, down_ref, rows_ref, more_ref, obs_ref):
    unpack_one(in_ref, up_ref, rows_ref, 32, 0)
    unpack_one(in_ref, obs_ref, more_ref, 32, 16)
    y = split(y_ref[...])
    for x in range(16):
        v = dot(split(up_ref[x, :64, :]), y)
        up_ref[x, :64, :] = v
        down_ref[x, :64, :] = v
        up_ref[x, 64:, :] = obs_ref[x, 32:, :]
        down_ref[x, 64:, :] = obs_ref[x, :32, :]


def pack_one(in_ref, out_ref, rows_ref, per, offset):
    for zc in range(8):
        for x in range(16):
            rows_ref[pl.ds(zc * 128 + x, 8, stride=16), :] = in_ref[x, zc * 8 : zc * 8 + 8, :]
    for zc in range(8):
        for half in range(2):
            at = zc * 128 + half * 8
            tiles = swap_groups([rows_ref[at + 16 * i : at + 16 * i + 8, :] for i in range(8)])
            at = zc * 8 * per + half * 8 + offset
            for i in range(8):
                out_ref[at + per * i : at + per * i + 8, :] = tiles[i]


def pack_kernel(in_ref, out_ref, rows_ref):
    pack_one(in_ref, out_ref, rows_ref, 16, 0)


def exchange(rows):
    per = rows.shape[0] // 64
    t = lax.all_to_all(rows.reshape(64, per, 128), SLAB, 0, 0, tiled=True)
    return t.reshape(rows.shape)


def tap_vectors(psf_ref, flip):
    total = psf_ref[0]
    for k in range(1, 31):
        total = total + psf_ref[k]
    scale = 1.0 / jnp.full((8, 128), total, jnp.float32)
    return [psf_ref[30 - k if flip else k] * scale for k in range(31)]


def add_block(w, ref, z, acc, shift):
    for j in range(16):
        v = ref[j, z, :]
        for i in range(16):
            k = j + shift - i + 15
            if 0 <= k <= 30:
                p = w[k] * v
                acc[i] = p if acc[i] is None else acc[i] + p
    return acc


def over_planes(body):
    def step(t, _):
        body(pl.ds(pl.multiple_of(t * 8, 8), 8))
        return 0

    lax.fori_loop(0, 8, step, 0)


def own_x_kernel(flip, psf_ref, own_ref, out_ref):
    w = tap_vectors(psf_ref, flip)

    def body(z):
        acc = add_block(w, own_ref, z, [None] * 16, 0)
        for i in range(16):
            out_ref[i, z, :] = acc[i]

    over_planes(body)


def add_side(w, core_ref, part_ref, side_ref, shift, finish):
    def run(shift):
        def body(z):
            acc = [part_ref[i, z, :] for i in range(16)]
            finish(z, add_block(w, side_ref, z, acc, shift))

        over_planes(body)

    pl.when(core_ref[0] == 0)(lambda: run(shift))
    pl.when(core_ref[0] != 0)(lambda: run(-shift))


def side_kernel(flip, shift, psf_ref, core_ref, part_ref, side_ref, out_ref):
    def finish(z, acc):
        for i in range(16):
            out_ref[i, z, :] = acc[i]

    add_side(tap_vectors(psf_ref, flip), core_ref, part_ref, side_ref, shift, finish)


def update_kernel(flip, psf_ref, core_ref, part_ref, side_ref, est_ref, y_ref, new_ref, out_ref):
    def finish(z, acc):
        for i in range(16):
            new_ref[i, z, :] = est_ref[i, z, :] * acc[i]

    add_side(tap_vectors(psf_ref, flip), core_ref, part_ref, side_ref, 16, finish)
    y = split(y_ref[...])
    for i in range(16):
        out_ref[i] = dot(split(new_ref[i]), y)


def x_halo(v, psf, core, flip, ride=None):
    passed = lax.ppermute(v, SLAB, NEXT)
    swapped = lax.ppermute(v, "c", SWAP)
    part = call(functools.partial(own_x_kernel, flip), BLOCK, [psf, v], 1.3, "x_own")
    if ride is not None:
        ride, part = lax.optimization_barrier((ride, part))
        ride = exchange(ride)
    kernel = functools.partial(side_kernel, flip, -16)
    part = call(kernel, BLOCK, [psf, core, part, passed], 1, "x_passed")
    return part, swapped, ride


def ratio_kernel(
    slab_ref, v_ref, below_ref, above_ref, obs_ref, zo_ref, zl_ref, zh_ref, za_ref, ya_ref,
    out_ref, ratio_ref
):
    has_below = jnp.full((32, 128), slab_ref[0], jnp.int32) > 0
    has_above = jnp.full((32, 128), slab_ref[0], jnp.int32) < 7
    own, low_band, high_band = split(zo_ref[...]), split(zl_ref[...]), split(zh_ref[...])
    adjoint, y = split(za_ref[...]), split(ya_ref[...])
    for x in range(16):
        part = dot(own, split(v_ref[x, :64, :]))
        low = part[:64] + dot(low_band, split(below_ref[x, :64, :]))
        high = part[64:] + dot(high_band, split(above_ref[x, :64, :]))
        ratio_ref[x, :32, :] = jnp.where(has_below, obs_ref[x, :32, :] / low[:32], 0.0)
        ratio_ref[x, 32:64, :] = obs_ref[x, 32:64, :] / low[32:]
        ratio_ref[x, 64:96, :] = obs_ref[x, 64:96, :] / high[:32]
        ratio_ref[x, 96:, :] = jnp.where(has_above, obs_ref[x, 96:, :] / high[32:], 0.0)
    for x in range(16):
        out_ref[x] = dot(split(dot(adjoint, split(ratio_ref[x]))), y)


def first_ratio_kernel(
    slab_ref, up_ref, down_ref, below_ref, above_ref, zo_ref, zl_ref, zh_ref, za_ref, ya_ref,
    out_ref, obs_ref, ratio_ref
):
    parts = (below_ref, down_ref, up_ref, above_ref)
    for i in range(4):
        obs_ref[:, 32 * i : 32 * i + 32, :] = parts[i][:, 64:, :]
    ratio_kernel(
        slab_ref, up_ref, below_ref, above_ref, obs_ref, zo_ref, zl_ref, zh_ref, za_ref, ya_ref,
        out_ref, ratio_ref
    )


def per_device(observed, estimate, psf_y, psf_x, psf_z):
    core = lax.axis_index("c").reshape(1)
    slab = lax.axis_index("z").reshape(1)
    est0 = estimate.reshape(128, 1024)

    first = pl.pallas_call(
        first_kernel,
        out_shape=pltpu.VMEM((2048, 128), jnp.float32),
        in_specs=[SMEM, HBM, HBM],
        out_specs=VMEM,
        scratch_shapes=[
            pltpu.VMEM((128, 1024), jnp.float32),
            pltpu.VMEM((128, 1024), jnp.float32),
            pltpu.SemaphoreType.DMA((16,)),
        ],
        compiler_params=pltpu.CompilerParams(vmem_limit_bytes=LIMIT),
        name="first",
    )(
        psf_x,
        pltpu.with_memory_space_constraint(est0, pltpu.HBM),
        pltpu.with_memory_space_constraint(observed.reshape(128, 1024), pltpu.HBM),
    )
    arrived = exchange(first)
    yf, ya, zo, zl, zh, za = prepare(psf_y, psf_z)
    turned = call(turn_kernel, ROWS, [est0], 1, "turn", free=(0,))

    mats = [zo, zl, zh, za, ya]
    out = [(16, 96, 128), (16, 96, 128)]
    up, down = call(arrive_kernel, out, [arrived, yf], 2, "arrive", [ROWS, ROWS, BLOCK])
    below = lax.ppermute(up, "z", UP)
    above = lax.ppermute(down, "z", DOWN)
    turned, up = lax.optimization_barrier((turned, up))
    rode = exchange(turned)
    back, obs = call(
        first_ratio_kernel,
        [BLOCK, (16, 128, 128)],
        [slab, up, down, below, above, *mats],
        100,
        "first_ratio",
        [(16, 128, 128)],
    )
    est = call(unpack_kernel, BLOCK, [rode], 1, "unpack", [ROWS])
    part, swapped, _ = x_halo(back, psf_x, core, True)
    est, v = call(
        functools.partial(update_kernel, True),
        [BLOCK, BLOCK],
        [psf_x, core, part, swapped, est, yf],
        2,
        "update",
    )
    est_rows = call(pack_kernel, ROWS, [est], 1, "pack_est", [ROWS])
    part, swapped, est_rows = x_halo(v, psf_x, core, False, est_rows)
    kernel = functools.partial(side_kernel, False, 16)
    v = call(kernel, BLOCK, [psf_x, core, part, swapped], 1, "x_swapped")

    below = lax.ppermute(v, "z", UP)
    above = lax.ppermute(v, "z", DOWN)
    back = call(
        ratio_kernel, BLOCK, [slab, v, below, above, obs, *mats], 4, "ratio", [(16, 128, 128)]
    )
    rows = exchange(call(pack_kernel, ROWS, [back], 1, "pack_back", [ROWS]))
    out = call(last_kernel, (128, 1024), [psf_x, rows, est_rows], 4, "last", free_out=True)
    return out.reshape(8, 16, 1024)


def solution(mesh):
    fine = Mesh(mesh.devices.reshape(8, 4, 2, 4, 2), ("z", "x", "yl", "yh", "c"))
    spec = P(("z", "x", "yl"), ("yh", "c"), None)
    return jax.shard_map(
        per_device,
        mesh=fine,
        in_specs=(spec, spec, P(), P(), P()),
        out_specs=spec,
        check_vma=False,
    )
```

```python
import functools

import jax
import jax.numpy as jnp
from jax import lax
from jax.experimental import pallas as pl
from jax.experimental.pallas import tpu as pltpu
from jax.sharding import Mesh, PartitionSpec as P

LIMIT = 6 * 2**20
SLAB = ("x", "yl", "yh", "c")
BLOCK = (16, 64, 128)
ROWS = (1024, 128)
VMEM = pl.BlockSpec(memory_space=pltpu.VMEM)
SMEM = pl.BlockSpec(memory_space=pltpu.SMEM)
HBM = pl.BlockSpec(memory_space=pltpu.HBM)


def x_index(b, c):
    x, yh, yl = b // 8, (b % 8) // 2, b % 2
    return ((x * 2 + yl) * 4 + yh) * 2 + c


SWAP = [(0, 1), (1, 0)]
NEXT = [(x_index(b, 0), x_index(b - 1, 1)) for b in range(1, 32)] + [
    (x_index(b, 1), x_index(b + 1, 0)) for b in range(31)
]
UP = [(z, z + 1) for z in range(7)]
DOWN = [(z + 1, z) for z in range(7)]


def is_shape(s):
    return isinstance(s, tuple)


def call(kernel, out, args, us, name, scratch=(), save=None):
    args = [a if a.ndim == 1 else pltpu.with_memory_space_constraint(a, pltpu.VMEM) for a in args]
    shapes = jax.tree.map(lambda s: pltpu.VMEM(s, jnp.float32), out, is_leaf=is_shape)
    specs = jax.tree.map(lambda s: VMEM, out, is_leaf=is_shape)
    scratch = [pltpu.VMEM(s, jnp.float32) for s in scratch]
    if save:
        shapes, specs = [shapes, pltpu.HBM(save, jnp.float32)], [specs, HBM]
        scratch.append(pltpu.SemaphoreType.DMA((2,)))
    return pl.pallas_call(
        kernel,
        out_shape=shapes,
        in_specs=[SMEM if a.ndim == 1 else VMEM for a in args],
        out_specs=specs,
        scratch_shapes=scratch,
        cost_estimate=pl.CostEstimate(
            flops=int(us * 1e9), bytes_accessed=int(us * 3e6), transcendentals=0
        ),
        compiler_params=pltpu.CompilerParams(vmem_limit_bytes=LIMIT),
        name=name,
    )(*args)


def split(m):
    high = m.astype(jnp.bfloat16)
    return high, (m - high.astype(jnp.float32)).astype(jnp.bfloat16)


def dot(a, b):
    (ah, al), (bh, bl) = a, b

    def one(p, q):
        return jnp.dot(p, q, preferred_element_type=jnp.float32)

    return one(ah, bh) + (one(al, bh) + one(ah, bl))


def band(psf_ref, lead, flip, rows):
    taps = psf_ref.shape[0]
    lane = lax.broadcasted_iota(jnp.int32, (8, 256), 1)
    line = jnp.zeros((8, 256), jnp.float32)
    total = psf_ref[0]
    for k in range(taps):
        if k:
            total = total + psf_ref[k]
        line = jnp.where(lane == (k + lead) % 256, psf_ref[taps - 1 - k if flip else k], line)
    line = line / jnp.full((8, 256), total, jnp.float32)
    return pltpu.roll(jnp.broadcast_to(line[:1], (rows, 256)), 0, 1, stride=1, stride_axis=0)


def x_band(psf_ref, flip):
    m = band(psf_ref, -15, not flip, 128)
    return m[:, :128], m[:, 128:]


def prep_kernel(
    psf_y_ref, psf_x_ref, psf_z_ref, yf_ref, ya_ref, xn_ref, xf_ref, zo_ref, zl_ref, zh_ref, za_ref
):
    yf_ref[...] = band(psf_y_ref, -15, True, 128)[:, :128]
    ya_ref[...] = band(psf_y_ref, -15, False, 128)[:, :128]
    xn_ref[...], xf_ref[...] = x_band(psf_x_ref, True)
    fwd = band(psf_z_ref, 1, False, 128)
    zl_ref[...] = fwd[:64, :64]
    zo_ref[...] = fwd[:, 64:128]
    zh_ref[...] = fwd[64:, 128:192]
    za_ref[...] = band(psf_z_ref, 1, True, 64)[:, :128]


def prepare(psf_y, psf_x, psf_z):
    out = [(128, 128)] * 4 + [(128, 64), (64, 64), (64, 64), (64, 128)]
    return call(prep_kernel, out, [psf_y, psf_x, psf_z], 1, "prepare")


def blur_lanes(tiles, near, far):
    lane = lax.broadcasted_iota(jnp.int32, tiles[0].shape, 1)
    zero = jnp.zeros_like(tiles[0])
    near, far = split(near), split(far)
    out = []
    for t in range(8):
        after = tiles[t + 1] if t < 7 else zero
        before = tiles[t - 1] if t > 0 else zero
        out.append(dot(split(tiles[t]), near) + dot(split(jnp.where(lane < 64, after, before)), far))
    return out


def rows_at(t, i, per=16, offset=0):
    block = 8 * t + i
    return x_index(block // 2, block % 2) * per + offset


def write_columns(out_ref, t, tile, per=16, offset=0):
    turned = tile.T
    for i in range(8):
        at = rows_at(t, i, per, offset)
        out_ref[at : at + 16, :] = turned[16 * i : 16 * i + 16, :]


def first_kernel(psf_x_hbm, est_hbm, obs_hbm, out_ref, est_ref, obs_ref, psf_x_ref, sems):
    taps = pltpu.make_async_copy(psf_x_hbm, psf_x_ref, sems.at[16])
    taps.start()
    copies = []
    for n, (src, dst) in enumerate(((est_hbm, est_ref), (obs_hbm, obs_ref))):
        for t in range(8):
            spot = pl.ds(128 * t, 128)
            copies.append(
                pltpu.make_async_copy(src.at[:, spot], dst.at[:, spot], sems.at[8 * n + t])
            )
            copies[-1].start()
    taps.wait()
    near, far = x_band(psf_x_ref, False)
    for copy in copies[:8]:
        copy.wait()
    blurred = blur_lanes([est_ref[:, 128 * t : 128 * t + 128] for t in range(8)], near, far)
    for t in range(8):
        write_columns(out_ref, t, blurred[t], 32, 0)
    for t in range(8):
        copies[8 + t].wait()
        write_columns(out_ref, t, obs_ref[:, 128 * t : 128 * t + 128], 32, 16)


def save_observed(low_ref, high_ref, out_hbm, sems):
    copies = [
        pltpu.make_async_copy(
            ref.at[:, pl.ds(64, 32), :], out_hbm.at[:, pl.ds(32 * i, 32), :], sems.at[i]
        )
        for i, ref in enumerate((low_ref, high_ref))
    ]
    for copy in copies:
        copy.start()
    return copies


def turn_kernel(in_ref, down_ref, up_ref, out_ref, obs_hbm, sems):
    copies = save_observed(down_ref, up_ref, obs_hbm, sems)
    for t in range(8):
        write_columns(out_ref, t, in_ref[:, 128 * t : 128 * t + 128])
    for copy in copies:
        copy.wait()


def last_kernel(back_ref, est_ref, near_ref, far_ref, out_hbm, out_ref, sems):
    def tile(ref, t):
        spots = [rows_at(t, i) for i in range(8)]
        return jnp.concatenate([ref[at : at + 16, :] for at in spots], axis=0).T

    blurred = blur_lanes([tile(back_ref, t) for t in range(8)], near_ref[...], far_ref[...])
    copies = []
    for t in range(8):
        spot = pl.ds(128 * t, 128)
        out_ref[:, spot] = blurred[t] * tile(est_ref, t)
        copies.append(pltpu.make_async_copy(out_ref.at[:, spot], out_hbm.at[:, spot], sems.at[t]))
        copies[t].start()
    for copy in copies:
        copy.wait()


def swap_groups(tiles):
    group = lax.broadcasted_iota(jnp.int32, (8, 128), 1) // 16
    tiles = [tiles[0]] + [pltpu.roll(tiles[i], 16 * i, 1) for i in range(1, 8)]
    for b in (1, 2, 4):
        taken = (group & b) != 0
        tiles = [jnp.where(taken, tiles[(i + b) % 8], tiles[i]) for i in range(8)]
    return [tiles[0]] + [pltpu.roll(tiles[8 - i], 128 - 16 * i, 1) for i in range(1, 8)]


def unpack_one(in_ref, out_ref, rows_ref, per, offset):
    for zc in range(8):
        for half in range(2):
            at = zc * 8 * per + half * 8 + offset
            tiles = swap_groups([in_ref[at + per * i : at + per * i + 8, :] for i in range(8)])
            at = zc * 128 + half * 8
            for i in range(8):
                rows_ref[at + 16 * i : at + 16 * i + 8, :] = tiles[i]
    for zc in range(8):
        for x in range(16):
            out_ref[x, zc * 8 : zc * 8 + 8, :] = rows_ref[pl.ds(zc * 128 + x, 8, stride=16), :]


def unpack_kernel(in_ref, out_ref, rows_ref):
    unpack_one(in_ref, out_ref, rows_ref, 16, 0)


def arrive_kernel(in_ref, y_ref, up_ref, down_ref, rows_ref, more_ref, obs_ref):
    unpack_one(in_ref, up_ref, rows_ref, 32, 0)
    unpack_one(in_ref, obs_ref, more_ref, 32, 16)
    y = split(y_ref[...])
    for x in range(16):
        v = dot(split(up_ref[x, :64, :]), y)
        up_ref[x, :64, :] = v
        down_ref[x, :64, :] = v
        up_ref[x, 64:, :] = obs_ref[x, 32:, :]
        down_ref[x, 64:, :] = obs_ref[x, :32, :]


def pack_one(in_ref, out_ref, rows_ref, per, offset):
    for zc in range(8):
        for x in range(16):
            rows_ref[pl.ds(zc * 128 + x, 8, stride=16), :] = in_ref[x, zc * 8 : zc * 8 + 8, :]
    for zc in range(8):
        for half in range(2):
            at = zc * 128 + half * 8
            tiles = swap_groups([rows_ref[at + 16 * i : at + 16 * i + 8, :] for i in range(8)])
            at = zc * 8 * per + half * 8 + offset
            for i in range(8):
                out_ref[at + per * i : at + per * i + 8, :] = tiles[i]


def pack_kernel(in_ref, out_ref, rows_ref):
    pack_one(in_ref, out_ref, rows_ref, 16, 0)


def exchange(rows):
    per = rows.shape[0] // 64
    t = lax.all_to_all(rows.reshape(64, per, 128), SLAB, 0, 0, tiled=True)
    return t.reshape(rows.shape)


def tap_vectors(psf_ref, flip):
    total = psf_ref[0]
    for k in range(1, 31):
        total = total + psf_ref[k]
    scale = 1.0 / jnp.full((8, 128), total, jnp.float32)
    return [psf_ref[30 - k if flip else k] * scale for k in range(31)]


def add_block(w, ref, z, acc, shift):
    for j in range(16):
        v = ref[j, z, :]
        for i in range(16):
            k = j + shift - i + 15
            if 0 <= k <= 30:
                p = w[k] * v
                acc[i] = p if acc[i] is None else acc[i] + p
    return acc


def over_planes(body):
    def step(t, _):
        body(pl.ds(pl.multiple_of(t * 8, 8), 8))
        return 0

    lax.fori_loop(0, 8, step, 0)


def own_x_kernel(flip, psf_ref, own_ref, out_ref):
    w = tap_vectors(psf_ref, flip)

    def body(z):
        acc = add_block(w, own_ref, z, [None] * 16, 0)
        for i in range(16):
            out_ref[i, z, :] = acc[i]

    over_planes(body)


def add_sides(w, core_ref, part_ref, passed_ref, swapped_ref, finish):
    def run(shift):
        def body(z):
            acc = [part_ref[i, z, :] for i in range(16)]
            acc = add_block(w, swapped_ref, z, acc, shift)
            finish(z, add_block(w, passed_ref, z, acc, -shift))

        over_planes(body)

    pl.when(core_ref[0] == 0)(lambda: run(16))
    pl.when(core_ref[0] != 0)(lambda: run(-16))


def sides_kernel(flip, psf_ref, core_ref, swapped_ref, passed_ref, part_ref, out_ref):
    def finish(z, acc):
        for i in range(16):
            out_ref[i, z, :] = acc[i]

    add_sides(tap_vectors(psf_ref, flip), core_ref, part_ref, passed_ref, swapped_ref, finish)


def update_kernel(flip, psf_ref, core_ref, swapped_ref, passed_ref, part_ref, est_ref, y_ref, new_ref, out_ref):
    y = split(y_ref[...])

    def finish(z, acc):
        for i in range(16):
            acc[i] = est_ref[i, z, :] * acc[i]
            new_ref[i, z, :] = acc[i]

    add_sides(tap_vectors(psf_ref, flip), core_ref, part_ref, passed_ref, swapped_ref, finish)
    for i in range(16):
        out_ref[i] = dot(split(new_ref[i]), y)


def x_halo(v, psf, flip, later):
    passed = lax.ppermute(v, SLAB, NEXT)
    swapped = lax.ppermute(v, "c", SWAP)
    part = call(functools.partial(own_x_kernel, flip), BLOCK, [psf, v], 1.3, "x_own")
    later, part = lax.optimization_barrier((later, part))
    return [swapped, passed, part], later


def ratio_planes(slab_ref, v_ref, below_ref, above_ref, obs, mats, out_ref, ratio_ref):
    has_below = jnp.full((32, 128), slab_ref[0], jnp.int32) > 0
    has_above = jnp.full((32, 128), slab_ref[0], jnp.int32) < 7
    own, low_band, high_band, adjoint, y = [split(m[...]) for m in mats]
    for x in range(16):
        part = dot(own, split(v_ref[x, :64, :]))
        low = part[:64] + dot(low_band, split(below_ref[x, :64, :]))
        high = part[64:] + dot(high_band, split(above_ref[x, :64, :]))
        ratio_ref[x, :32, :] = jnp.where(has_below, obs(0, x) / low[:32], 0.0)
        ratio_ref[x, 32:64, :] = obs(1, x) / low[32:]
        ratio_ref[x, 64:96, :] = obs(2, x) / high[:32]
        ratio_ref[x, 96:, :] = jnp.where(has_above, obs(3, x) / high[32:], 0.0)
    for x in range(16):
        out_ref[x] = dot(split(dot(adjoint, split(ratio_ref[x]))), y)


def ratio_kernel(slab_ref, v_ref, below_ref, above_ref, obs_ref, halo_ref, *refs):
    *mats, out_ref, ratio_ref, back_ref, rows_ref = refs

    def obs(i, x):
        ref, at = ((halo_ref, 0), (obs_ref, 0), (obs_ref, 32), (halo_ref, 32))[i]
        return ref[x, at : at + 32, :]

    ratio_planes(slab_ref, v_ref, below_ref, above_ref, obs, mats, back_ref, ratio_ref)
    pack_one(back_ref, out_ref, rows_ref, 16, 0)


def first_ratio_kernel(slab_ref, up_ref, down_ref, below_ref, above_ref, *refs):
    *mats, out_ref, halo_hbm, ratio_ref, sems = refs
    parts = (below_ref, down_ref, up_ref, above_ref)
    copies = save_observed(below_ref, above_ref, halo_hbm, sems)

    def obs(i, x):
        return parts[i][x, 64:, :]

    ratio_planes(slab_ref, up_ref, below_ref, above_ref, obs, mats, out_ref, ratio_ref)
    for copy in copies:
        copy.wait()


def per_device(observed, estimate, psf_y, psf_x, psf_z):
    core = lax.axis_index("c").reshape(1)
    slab = lax.axis_index("z").reshape(1)
    est0, obs0 = estimate.reshape(128, 1024), observed.reshape(128, 1024)

    first = pl.pallas_call(
        first_kernel,
        out_shape=pltpu.VMEM((2048, 128), jnp.float32),
        in_specs=[HBM, HBM, HBM],
        out_specs=VMEM,
        scratch_shapes=[
            pltpu.VMEM((128, 1024), jnp.float32),
            pltpu.VMEM((128, 1024), jnp.float32),
            pltpu.SMEM((31,), jnp.float32),
            pltpu.SemaphoreType.DMA((17,)),
        ],
        compiler_params=pltpu.CompilerParams(vmem_limit_bytes=LIMIT),
        name="first",
    )(*[pltpu.with_memory_space_constraint(a, pltpu.HBM) for a in (psf_x, est0, obs0)])
    arrived = exchange(first)
    yf, ya, xn, xf, zo, zl, zh, za = prepare(psf_y, psf_x, psf_z)
    mats = [zo, zl, zh, za, ya]
    out = [(16, 96, 128), (16, 96, 128)]
    up, down = call(arrive_kernel, out, [arrived, yf], 2, "arrive", [ROWS, ROWS, BLOCK])
    below = lax.ppermute(up, "z", UP)
    above = lax.ppermute(down, "z", DOWN)
    turned, obs = call(turn_kernel, ROWS, [est0, down, up], 1, "turn", save=BLOCK)
    rode = exchange(turned)
    args = [slab, up, down, below, above, *mats]
    scratch = [(16, 128, 128)]
    back, halo = call(first_ratio_kernel, BLOCK, args, 100, "first_ratio", scratch, BLOCK)
    est = call(unpack_kernel, BLOCK, [rode], 1, "unpack", [ROWS])
    sides, _ = x_halo(back, psf_x, True, ())
    est, v = call(
        functools.partial(update_kernel, True),
        [BLOCK, BLOCK],
        [psf_x, core, *sides, est, yf],
        2,
        "update",
    )
    est_rows = call(pack_kernel, ROWS, [est], 1, "pack_est", [ROWS])
    sides, est_rows = x_halo(v, psf_x, False, est_rows)
    est_rows = exchange(est_rows)
    v = call(functools.partial(sides_kernel, False), BLOCK, [psf_x, core, *sides], 1, "x_sides")

    below = lax.ppermute(v, "z", UP)
    above = lax.ppermute(v, "z", DOWN)
    scratch = [(16, 128, 128), BLOCK, ROWS]
    rows = call(ratio_kernel, ROWS, [slab, v, below, above, obs, halo, *mats], 4, "ratio", scratch)
    rows = exchange(rows)
    out = pl.pallas_call(
        last_kernel,
        out_shape=pltpu.HBM((128, 1024), jnp.float32),
        in_specs=[VMEM] * 4,
        out_specs=HBM,
        scratch_shapes=[pltpu.VMEM((128, 1024), jnp.float32), pltpu.SemaphoreType.DMA((8,))],
        compiler_params=pltpu.CompilerParams(vmem_limit_bytes=LIMIT),
        name="last",
    )(*[pltpu.with_memory_space_constraint(a, pltpu.VMEM) for a in (rows, est_rows, xn, xf)])
    return out.reshape(8, 16, 1024)


def solution(mesh):
    fine = Mesh(mesh.devices.reshape(8, 4, 2, 4, 2), ("z", "x", "yl", "yh", "c"))
    spec = P(("z", "x", "yl"), ("yh", "c"), None)
    return jax.shard_map(
        per_device,
        mesh=fine,
        in_specs=(spec, spec, P(), P(), P()),
        out_specs=spec,
        check_vma=False,
    )
```

```python
import functools

import jax
import jax.numpy as jnp
from jax import lax
from jax.experimental import pallas as pl
from jax.experimental.pallas import tpu as pltpu
from jax.sharding import Mesh, PartitionSpec as P

LIMIT = 6 * 2**20
SLAB = ("x", "yl", "yh", "c")
BLOCK = (16, 64, 128)
ROWS = (1024, 128)
VMEM = pl.BlockSpec(memory_space=pltpu.VMEM)
SMEM = pl.BlockSpec(memory_space=pltpu.SMEM)
HBM = pl.BlockSpec(memory_space=pltpu.HBM)


def x_index(b, c):
    x, yh, yl = b // 8, (b % 8) // 2, b % 2
    return ((x * 2 + yl) * 4 + yh) * 2 + c


SWAP = [(0, 1), (1, 0)]
NEXT = [(x_index(b, 0), x_index(b - 1, 1)) for b in range(1, 32)] + [
    (x_index(b, 1), x_index(b + 1, 0)) for b in range(31)
]
UP = [(z, z + 1) for z in range(7)]
DOWN = [(z + 1, z) for z in range(7)]


def is_shape(s):
    return isinstance(s, tuple)


def call(kernel, out, args, us, name, scratch=(), save=None):
    args = [a if a.ndim == 1 else pltpu.with_memory_space_constraint(a, pltpu.VMEM) for a in args]
    shapes = jax.tree.map(lambda s: pltpu.VMEM(s, jnp.float32), out, is_leaf=is_shape)
    specs = jax.tree.map(lambda s: VMEM, out, is_leaf=is_shape)
    scratch = [pltpu.VMEM(s, jnp.float32) for s in scratch]
    if save:
        shapes = [*(shapes if isinstance(shapes, list) else [shapes]), pltpu.HBM(save, jnp.float32)]
        specs = [*(specs if isinstance(specs, list) else [specs]), HBM]
        scratch.append(pltpu.SemaphoreType.DMA((2,)))
    return pl.pallas_call(
        kernel,
        out_shape=shapes,
        in_specs=[SMEM if a.ndim == 1 else VMEM for a in args],
        out_specs=specs,
        scratch_shapes=scratch,
        cost_estimate=pl.CostEstimate(
            flops=int(us * 1e9), bytes_accessed=int(us * 3e6), transcendentals=0
        ),
        compiler_params=pltpu.CompilerParams(vmem_limit_bytes=LIMIT),
        name=name,
    )(*args)


def split(m):
    high = m.astype(jnp.bfloat16)
    return high, (m - high.astype(jnp.float32)).astype(jnp.bfloat16)


def dot(a, b):
    (ah, al), (bh, bl) = a, b

    def one(p, q):
        return jnp.dot(p, q, preferred_element_type=jnp.float32)

    return one(ah, bh) + (one(al, bh) + one(ah, bl))


def band(psf_ref, lead, flip, rows):
    taps = psf_ref.shape[0]
    lane = lax.broadcasted_iota(jnp.int32, (8, 256), 1)
    line = jnp.zeros((8, 256), jnp.float32)
    total = psf_ref[0]
    for k in range(taps):
        if k:
            total = total + psf_ref[k]
        line = jnp.where(lane == (k + lead) % 256, psf_ref[taps - 1 - k if flip else k], line)
    line = line / jnp.full((8, 256), total, jnp.float32)
    return pltpu.roll(jnp.broadcast_to(line[:1], (rows, 256)), 0, 1, stride=1, stride_axis=0)


def x_band(psf_ref, flip):
    m = band(psf_ref, -15, not flip, 128)
    return m[:, :128], m[:, 128:]


def prep_kernel(
    psf_y_ref, psf_x_ref, psf_z_ref, yf_ref, ya_ref, xn_ref, xf_ref, zo_ref, zl_ref, zh_ref, al_ref, ah_ref
):
    yf_ref[...] = band(psf_y_ref, -15, True, 128)[:, :128]
    ya_ref[...] = band(psf_y_ref, -15, False, 128)[:, :128]
    xn_ref[...], xf_ref[...] = x_band(psf_x_ref, True)
    fwd = band(psf_z_ref, 1, False, 128)
    zl_ref[...] = fwd[:64, :64]
    zo_ref[...] = fwd[:, 64:128]
    zh_ref[...] = fwd[64:, 128:192]
    adjoint = band(psf_z_ref, 1, True, 64)
    al_ref[...], ah_ref[...] = adjoint[:, :64], adjoint[:, 64:128]


def prepare(psf_y, psf_x, psf_z):
    out = [(128, 128)] * 4 + [(128, 64)] + [(64, 64)] * 4
    return call(prep_kernel, out, [psf_y, psf_x, psf_z], 1, "prepare")


def blur_lanes(tiles, near, far):
    lane = lax.broadcasted_iota(jnp.int32, tiles[0].shape, 1)
    zero = jnp.zeros_like(tiles[0])
    near, far = split(near), split(far)
    out = []
    for t in range(8):
        after = tiles[t + 1] if t < 7 else zero
        before = tiles[t - 1] if t > 0 else zero
        out.append(dot(split(tiles[t]), near) + dot(split(jnp.where(lane < 64, after, before)), far))
    return out


def rows_at(t, i, per=16, offset=0):
    block = 8 * t + i
    return x_index(block // 2, block % 2) * per + offset


def write_columns(out_ref, t, tile, per=16, offset=0):
    turned = tile.T
    for i in range(8):
        at = rows_at(t, i, per, offset)
        out_ref[at : at + 16, :] = turned[16 * i : 16 * i + 16, :]


def first_kernel(psf_x_hbm, est_hbm, obs_hbm, out_ref, est_ref, obs_ref, psf_x_ref, sems):
    taps = pltpu.make_async_copy(psf_x_hbm, psf_x_ref, sems.at[16])
    taps.start()
    copies = []
    for n, (src, dst) in enumerate(((est_hbm, est_ref), (obs_hbm, obs_ref))):
        for t in range(8):
            spot = pl.ds(128 * t, 128)
            copies.append(
                pltpu.make_async_copy(src.at[:, spot], dst.at[:, spot], sems.at[8 * n + t])
            )
            copies[-1].start()
    taps.wait()
    near, far = x_band(psf_x_ref, False)
    for copy in copies[:8]:
        copy.wait()
    blurred = blur_lanes([est_ref[:, 128 * t : 128 * t + 128] for t in range(8)], near, far)
    for t in range(8):
        write_columns(out_ref, t, blurred[t], 32, 0)
    for t in range(8):
        copies[8 + t].wait()
        write_columns(out_ref, t, obs_ref[:, 128 * t : 128 * t + 128], 32, 16)


def save_observed(refs, out_hbm, sems):
    copies = [
        pltpu.make_async_copy(
            ref.at[:, pl.ds(64, 32), :], out_hbm.at[:, pl.ds(32 * i, 32), :], sems.at[i]
        )
        for i, ref in enumerate(refs)
    ]
    for copy in copies:
        copy.start()
    return copies


def turn_kernel(in_ref, down_ref, up_ref, out_ref, obs_hbm, sems):
    copies = save_observed([down_ref, up_ref], obs_hbm, sems)
    for t in range(8):
        write_columns(out_ref, t, in_ref[:, 128 * t : 128 * t + 128])
    for copy in copies:
        copy.wait()


def last_kernel(back_ref, est_ref, near_ref, far_ref, out_hbm, out_ref, sems):
    def tile(ref, t):
        spots = [rows_at(t, i) for i in range(8)]
        return jnp.concatenate([ref[at : at + 16, :] for at in spots], axis=0).T

    blurred = blur_lanes([tile(back_ref, t) for t in range(8)], near_ref[...], far_ref[...])
    copies = []
    for t in range(8):
        spot = pl.ds(128 * t, 128)
        out_ref[:, spot] = blurred[t] * tile(est_ref, t)
        copies.append(pltpu.make_async_copy(out_ref.at[:, spot], out_hbm.at[:, spot], sems.at[t]))
        copies[t].start()
    for copy in copies:
        copy.wait()


def swap_groups(tiles):
    group = lax.broadcasted_iota(jnp.int32, (8, 128), 1) // 16
    tiles = [tiles[0]] + [pltpu.roll(tiles[i], 16 * i, 1) for i in range(1, 8)]
    for b in (1, 2, 4):
        taken = (group & b) != 0
        tiles = [jnp.where(taken, tiles[(i + b) % 8], tiles[i]) for i in range(8)]
    return [tiles[0]] + [pltpu.roll(tiles[8 - i], 128 - 16 * i, 1) for i in range(1, 8)]


def unpack_one(in_ref, out_ref, rows_ref, per, offset):
    for zc in range(8):
        for half in range(2):
            at = zc * 8 * per + half * 8 + offset
            tiles = swap_groups([in_ref[at + per * i : at + per * i + 8, :] for i in range(8)])
            at = zc * 128 + half * 8
            for i in range(8):
                rows_ref[at + 16 * i : at + 16 * i + 8, :] = tiles[i]
    for zc in range(8):
        for x in range(16):
            out_ref[x, zc * 8 : zc * 8 + 8, :] = rows_ref[pl.ds(zc * 128 + x, 8, stride=16), :]


def unpack_kernel(in_ref, out_ref, rows_ref):
    unpack_one(in_ref, out_ref, rows_ref, 16, 0)


def arrive_kernel(in_ref, y_ref, up_ref, down_ref, rows_ref, more_ref, obs_ref):
    unpack_one(in_ref, up_ref, rows_ref, 32, 0)
    unpack_one(in_ref, obs_ref, more_ref, 32, 16)
    y = split(y_ref[...])
    for x in range(16):
        v = dot(split(up_ref[x, :64, :]), y)
        up_ref[x, :64, :] = v
        down_ref[x, :64, :] = v
        up_ref[x, 64:, :] = obs_ref[x, 32:, :]
        down_ref[x, 64:, :] = obs_ref[x, :32, :]


def pack_one(in_ref, out_ref, rows_ref, per, offset):
    for zc in range(8):
        for x in range(16):
            rows_ref[pl.ds(zc * 128 + x, 8, stride=16), :] = in_ref[x, zc * 8 : zc * 8 + 8, :]
    for zc in range(8):
        for half in range(2):
            at = zc * 128 + half * 8
            tiles = swap_groups([rows_ref[at + 16 * i : at + 16 * i + 8, :] for i in range(8)])
            at = zc * 8 * per + half * 8 + offset
            for i in range(8):
                out_ref[at + per * i : at + per * i + 8, :] = tiles[i]


def pack_kernel(in_ref, out_ref, rows_ref):
    pack_one(in_ref, out_ref, rows_ref, 16, 0)


def exchange(rows):
    per = rows.shape[0] // 64
    t = lax.all_to_all(rows.reshape(64, per, 128), SLAB, 0, 0, tiled=True)
    return t.reshape(rows.shape)


def tap_vectors(psf_ref, flip):
    total = psf_ref[0]
    for k in range(1, 31):
        total = total + psf_ref[k]
    scale = 1.0 / jnp.full((8, 128), total, jnp.float32)
    return [psf_ref[30 - k if flip else k] * scale for k in range(31)]


def add_block(w, ref, z, acc, shift):
    for j in range(16):
        v = ref[j, z, :]
        for i in range(16):
            k = j + shift - i + 15
            if 0 <= k <= 30:
                p = w[k] * v
                acc[i] = p if acc[i] is None else acc[i] + p
    return acc


def over_planes(body):
    def step(t, _):
        body(pl.ds(pl.multiple_of(t * 8, 8), 8))
        return 0

    lax.fori_loop(0, 8, step, 0)


def own_x_kernel(flip, psf_ref, own_ref, out_ref):
    w = tap_vectors(psf_ref, flip)

    def body(z):
        acc = add_block(w, own_ref, z, [None] * 16, 0)
        for i in range(16):
            out_ref[i, z, :] = acc[i]

    over_planes(body)


def add_sides(w, core_ref, part_ref, passed_ref, swapped_ref, finish):
    def run(shift):
        def body(z):
            acc = [part_ref[i, z, :] for i in range(16)]
            acc = add_block(w, swapped_ref, z, acc, shift)
            finish(z, add_block(w, passed_ref, z, acc, -shift))

        over_planes(body)

    pl.when(core_ref[0] == 0)(lambda: run(16))
    pl.when(core_ref[0] != 0)(lambda: run(-16))


def sides_kernel(flip, psf_ref, core_ref, swapped_ref, passed_ref, part_ref, out_ref):
    def finish(z, acc):
        for i in range(16):
            out_ref[i, z, :] = acc[i]

    add_sides(tap_vectors(psf_ref, flip), core_ref, part_ref, passed_ref, swapped_ref, finish)


def update_kernel(flip, psf_ref, core_ref, swapped_ref, passed_ref, part_ref, est_ref, y_ref, new_ref, out_ref):
    y = split(y_ref[...])

    def finish(z, acc):
        for i in range(16):
            acc[i] = est_ref[i, z, :] * acc[i]
            new_ref[i, z, :] = acc[i]

    add_sides(tap_vectors(psf_ref, flip), core_ref, part_ref, passed_ref, swapped_ref, finish)
    for i in range(16):
        out_ref[i] = dot(split(new_ref[i]), y)


def x_halo(v, psf, flip, later):
    passed = lax.ppermute(v, SLAB, NEXT)
    swapped = lax.ppermute(v, "c", SWAP)
    part = call(functools.partial(own_x_kernel, flip), BLOCK, [psf, v], 1.3, "x_own")
    later, part = lax.optimization_barrier((later, part))
    return [swapped, passed, part], later


def high_planes(slab_ref, v_ref, above_ref, obs, mats, sum_ref, low_ref):
    has_above = jnp.full((32, 128), slab_ref[0], jnp.int32) < 7
    own, band, adjoint = [split(m[...]) for m in mats]
    for x in range(16):
        part = dot(own, split(v_ref[x, :64, :]))
        low_ref[x] = part[:64]
        sum_ref[x] = part[64:] + dot(band, split(above_ref[x, :64, :]))
    for x in range(16):
        sum_ref[x, :32, :] = obs(2, x) / sum_ref[x, :32, :]
        sum_ref[x, 32:, :] = jnp.where(has_above, obs(3, x) / sum_ref[x, 32:, :], 0.0)
    for x in range(16):
        sum_ref[x] = dot(adjoint, split(sum_ref[x]))


def low_planes(slab_ref, low_ref, sum_ref, below_ref, obs, mats, out_ref):
    has_below = jnp.full((32, 128), slab_ref[0], jnp.int32) > 0
    band, adjoint, y = [split(m[...]) for m in mats]
    for x in range(16):
        out_ref[x] = low_ref[x] + dot(band, split(below_ref[x, :64, :]))
    for x in range(16):
        out_ref[x, :32, :] = jnp.where(has_below, obs(0, x) / out_ref[x, :32, :], 0.0)
        out_ref[x, 32:, :] = obs(1, x) / out_ref[x, 32:, :]
    for x in range(16):
        out_ref[x] = sum_ref[x] + dot(adjoint, split(out_ref[x]))
    for x in range(16):
        out_ref[x] = dot(split(out_ref[x]), y)


def first_high_kernel(slab_ref, up_ref, above_ref, zo_ref, zh_ref, ah_ref, *refs):
    sum_ref, low_ref, halo_hbm, sems = refs
    copies = save_observed([above_ref], halo_hbm, sems)

    def obs(i, x):
        return (up_ref, above_ref)[i - 2][x, 64:, :]

    high_planes(slab_ref, up_ref, above_ref, obs, (zo_ref, zh_ref, ah_ref), sum_ref, low_ref)
    for copy in copies:
        copy.wait()


def first_low_kernel(slab_ref, low_ref, sum_ref, down_ref, below_ref, zl_ref, al_ref, ya_ref, *refs):
    out_ref, halo_hbm, sems = refs
    copies = save_observed([below_ref], halo_hbm, sems)

    def obs(i, x):
        return (below_ref, down_ref)[i][x, 64:, :]

    low_planes(slab_ref, low_ref, sum_ref, below_ref, obs, (zl_ref, al_ref, ya_ref), out_ref)
    for copy in copies:
        copy.wait()


def high_kernel(
    slab_ref, v_ref, above_ref, halo_ref, obs_ref, zo_ref, zh_ref, ah_ref, sum_ref, low_ref
):
    def obs(i, x):
        return obs_ref[x, 32:, :] if i == 2 else halo_ref[x]

    high_planes(slab_ref, v_ref, above_ref, obs, (zo_ref, zh_ref, ah_ref), sum_ref, low_ref)


def low_kernel(
    slab_ref, low_ref, sum_ref, below_ref, obs_ref, halo_ref, zl_ref, al_ref, ya_ref,
    out_ref, back_ref, rows_ref
):
    def obs(i, x):
        return obs_ref[x, :32, :] if i else halo_ref[x]

    low_planes(slab_ref, low_ref, sum_ref, below_ref, obs, (zl_ref, al_ref, ya_ref), back_ref)
    pack_one(back_ref, out_ref, rows_ref, 16, 0)


def per_device(observed, estimate, psf_y, psf_x, psf_z):
    core = lax.axis_index("c").reshape(1)
    slab = lax.axis_index("z").reshape(1)
    est0, obs0 = estimate.reshape(128, 1024), observed.reshape(128, 1024)

    first = pl.pallas_call(
        first_kernel,
        out_shape=pltpu.VMEM((2048, 128), jnp.float32),
        in_specs=[HBM, HBM, HBM],
        out_specs=VMEM,
        scratch_shapes=[
            pltpu.VMEM((128, 1024), jnp.float32),
            pltpu.VMEM((128, 1024), jnp.float32),
            pltpu.SMEM((31,), jnp.float32),
            pltpu.SemaphoreType.DMA((17,)),
        ],
        compiler_params=pltpu.CompilerParams(vmem_limit_bytes=LIMIT),
        name="first",
    )(*[pltpu.with_memory_space_constraint(a, pltpu.HBM) for a in (psf_x, est0, obs0)])
    arrived = exchange(first)
    yf, ya, xn, xf, zo, zl, zh, al, ah = prepare(psf_y, psf_x, psf_z)
    low_mats, high_mats = [zl, al, ya], [zo, zh, ah]
    halo = (16, 32, 128)
    out = [(16, 96, 128), (16, 96, 128)]
    up, down = call(arrive_kernel, out, [arrived, yf], 2, "arrive", [ROWS, ROWS, BLOCK])
    below = lax.ppermute(up, "z", UP)
    above = lax.ppermute(down, "z", DOWN)
    turned, obs = call(turn_kernel, ROWS, [est0, down, up], 1, "turn", save=BLOCK)
    rode = exchange(turned)
    args = [slab, up, above, *high_mats]
    total, low, halo_above = call(
        first_high_kernel, [BLOCK, BLOCK], args, 1, "first_high", save=halo
    )
    args = [slab, low, total, down, below, *low_mats]
    back, halo_below = call(first_low_kernel, BLOCK, args, 100, "first_low", save=halo)
    est = call(unpack_kernel, BLOCK, [rode], 1, "unpack", [ROWS])
    sides, _ = x_halo(back, psf_x, True, ())
    est, v = call(
        functools.partial(update_kernel, True),
        [BLOCK, BLOCK],
        [psf_x, core, *sides, est, yf],
        2,
        "update",
    )
    est_rows = call(pack_kernel, ROWS, [est], 1, "pack_est", [ROWS])
    sides, est_rows = x_halo(v, psf_x, False, est_rows)
    est_rows = exchange(est_rows)
    v = call(functools.partial(sides_kernel, False), BLOCK, [psf_x, core, *sides], 1, "x_sides")

    below = lax.ppermute(v, "z", UP)
    above = lax.ppermute(v, "z", DOWN)
    args = [slab, v, above, halo_above, obs, *high_mats]
    total, low = call(high_kernel, [BLOCK, BLOCK], args, 1, "ratio_high")
    args = [slab, low, total, below, obs, halo_below, *low_mats]
    rows = call(low_kernel, ROWS, args, 4, "ratio_low", [BLOCK, ROWS])
    rows = exchange(rows)
    out = pl.pallas_call(
        last_kernel,
        out_shape=pltpu.HBM((128, 1024), jnp.float32),
        in_specs=[VMEM] * 4,
        out_specs=HBM,
        scratch_shapes=[pltpu.VMEM((128, 1024), jnp.float32), pltpu.SemaphoreType.DMA((8,))],
        compiler_params=pltpu.CompilerParams(vmem_limit_bytes=LIMIT),
        name="last",
    )(*[pltpu.with_memory_space_constraint(a, pltpu.VMEM) for a in (rows, est_rows, xn, xf)])
    return out.reshape(8, 16, 1024)


def solution(mesh):
    fine = Mesh(mesh.devices.reshape(8, 4, 2, 4, 2), ("z", "x", "yl", "yh", "c"))
    spec = P(("z", "x", "yl"), ("yh", "c"), None)
    return jax.shard_map(
        per_device,
        mesh=fine,
        in_specs=(spec, spec, P(), P(), P()),
        out_specs=spec,
        check_vma=False,
    )
```

```python
import functools

import jax
import jax.numpy as jnp
from jax import lax
from jax.experimental import pallas as pl
from jax.experimental.pallas import tpu as pltpu
from jax.sharding import Mesh, PartitionSpec as P

LIMIT = 6 * 2**20
SLAB = ("x", "yl", "yh", "c")
BLOCK = (16, 64, 128)
ROWS = (1024, 128)
VMEM = pl.BlockSpec(memory_space=pltpu.VMEM)
SMEM = pl.BlockSpec(memory_space=pltpu.SMEM)
HBM = pl.BlockSpec(memory_space=pltpu.HBM)


def x_index(b, c):
    x, yh, yl = b // 8, (b % 8) // 2, b % 2
    return ((x * 2 + yl) * 4 + yh) * 2 + c


SWAP = [(0, 1), (1, 0)]
NEXT = [(x_index(b, 0), x_index(b - 1, 1)) for b in range(1, 32)] + [
    (x_index(b, 1), x_index(b + 1, 0)) for b in range(31)
]
UP = [(z, z + 1) for z in range(7)]
DOWN = [(z + 1, z) for z in range(7)]


def is_shape(s):
    return isinstance(s, tuple)


def call(kernel, out, args, us, name, scratch=(), save=None):
    args = [a if a.ndim == 1 else pltpu.with_memory_space_constraint(a, pltpu.VMEM) for a in args]
    shapes = jax.tree.map(lambda s: pltpu.VMEM(s, jnp.float32), out, is_leaf=is_shape)
    specs = jax.tree.map(lambda s: VMEM, out, is_leaf=is_shape)
    scratch = [pltpu.VMEM(s, jnp.float32) for s in scratch]
    if save:
        shapes = [*(shapes if isinstance(shapes, list) else [shapes]), pltpu.HBM(save, jnp.float32)]
        specs = [*(specs if isinstance(specs, list) else [specs]), HBM]
        scratch.append(pltpu.SemaphoreType.DMA((2,)))
    return pl.pallas_call(
        kernel,
        out_shape=shapes,
        in_specs=[SMEM if a.ndim == 1 else VMEM for a in args],
        out_specs=specs,
        scratch_shapes=scratch,
        cost_estimate=pl.CostEstimate(
            flops=int(us * 1e9), bytes_accessed=int(us * 3e6), transcendentals=0
        ),
        compiler_params=pltpu.CompilerParams(vmem_limit_bytes=LIMIT),
        name=name,
    )(*args)


def split(m):
    high = m.astype(jnp.bfloat16)
    return high, (m - high.astype(jnp.float32)).astype(jnp.bfloat16)


def dot(a, b):
    (ah, al), (bh, bl) = a, b

    def one(p, q):
        return jnp.dot(p, q, preferred_element_type=jnp.float32)

    return one(ah, bh) + (one(al, bh) + one(ah, bl))


def band(psf_ref, lead, flip, rows):
    taps = psf_ref.shape[0]
    lane = lax.broadcasted_iota(jnp.int32, (8, 256), 1)
    line = jnp.zeros((8, 256), jnp.float32)
    total = psf_ref[0]
    for k in range(taps):
        if k:
            total = total + psf_ref[k]
        line = jnp.where(lane == (k + lead) % 256, psf_ref[taps - 1 - k if flip else k], line)
    line = line / jnp.full((8, 256), total, jnp.float32)
    return pltpu.roll(jnp.broadcast_to(line[:1], (rows, 256)), 0, 1, stride=1, stride_axis=0)


def x_band(psf_ref, flip):
    m = band(psf_ref, -15, not flip, 128)
    return m[:, :128], m[:, 128:]


def prep_kernel(
    psf_y_ref, psf_x_ref, psf_z_ref, yf_ref, ya_ref, xn_ref, xf_ref, zo_ref, zl_ref, zh_ref, al_ref, ah_ref
):
    yf_ref[...] = band(psf_y_ref, -15, True, 128)[:, :128]
    ya_ref[...] = band(psf_y_ref, -15, False, 128)[:, :128]
    xn_ref[...], xf_ref[...] = x_band(psf_x_ref, True)
    fwd = band(psf_z_ref, 1, False, 128)
    zl_ref[...] = fwd[:64, :64]
    zo_ref[...] = fwd[:, 64:128]
    zh_ref[...] = fwd[64:, 128:192]
    adjoint = band(psf_z_ref, 1, True, 64)
    al_ref[...], ah_ref[...] = adjoint[:, :64], adjoint[:, 64:128]


def prepare(psf_y, psf_x, psf_z):
    out = [(128, 128)] * 4 + [(128, 64)] + [(64, 64)] * 4
    return call(prep_kernel, out, [psf_y, psf_x, psf_z], 1, "prepare")


def blur_lanes(tiles, near, far):
    lane = lax.broadcasted_iota(jnp.int32, tiles[0].shape, 1)
    zero = jnp.zeros_like(tiles[0])
    near, far = split(near), split(far)
    out = []
    for t in range(8):
        after = tiles[t + 1] if t < 7 else zero
        before = tiles[t - 1] if t > 0 else zero
        out.append(dot(split(tiles[t]), near) + dot(split(jnp.where(lane < 64, after, before)), far))
    return out


def rows_at(t, i, per=16, offset=0):
    block = 8 * t + i
    return x_index(block // 2, block % 2) * per + offset


def write_columns(out_ref, t, tile, per=16, offset=0):
    turned = tile.T
    for i in range(8):
        at = rows_at(t, i, per, offset)
        out_ref[at : at + 16, :] = turned[16 * i : 16 * i + 16, :]


def first_kernel(psf_x_hbm, est_hbm, obs_hbm, out_ref, est_ref, obs_ref, psf_x_ref, sems):
    taps = pltpu.make_async_copy(psf_x_hbm, psf_x_ref, sems.at[16])
    taps.start()
    copies = []
    for n, (src, dst) in enumerate(((est_hbm, est_ref), (obs_hbm, obs_ref))):
        for t in range(8):
            spot = pl.ds(128 * t, 128)
            copies.append(
                pltpu.make_async_copy(src.at[:, spot], dst.at[:, spot], sems.at[8 * n + t])
            )
            copies[-1].start()
    taps.wait()
    near, far = x_band(psf_x_ref, False)
    for copy in copies[:8]:
        copy.wait()
    blurred = blur_lanes([est_ref[:, 128 * t : 128 * t + 128] for t in range(8)], near, far)
    for t in range(8):
        write_columns(out_ref, t, blurred[t], 32, 0)
    for t in range(8):
        copies[8 + t].wait()
        write_columns(out_ref, t, obs_ref[:, 128 * t : 128 * t + 128], 32, 16)


def save_observed(refs, out_hbm, sems):
    copies = [
        pltpu.make_async_copy(
            ref.at[:, pl.ds(64, 32), :], out_hbm.at[:, pl.ds(32 * i, 32), :], sems.at[i]
        )
        for i, ref in enumerate(refs)
    ]
    for copy in copies:
        copy.start()
    return copies


def turn_kernel(in_ref, down_ref, up_ref, out_ref, obs_hbm, sems):
    copies = save_observed([down_ref, up_ref], obs_hbm, sems)
    for t in range(8):
        write_columns(out_ref, t, in_ref[:, 128 * t : 128 * t + 128])
    for copy in copies:
        copy.wait()


def last_kernel(back_ref, est_ref, near_ref, far_ref, out_hbm, out_ref, sems):
    def tile(ref, t):
        spots = [rows_at(t, i) for i in range(8)]
        return jnp.concatenate([ref[at : at + 16, :] for at in spots], axis=0).T

    blurred = blur_lanes([tile(back_ref, t) for t in range(8)], near_ref[...], far_ref[...])
    copies = []
    for t in range(8):
        spot = pl.ds(128 * t, 128)
        out_ref[:, spot] = blurred[t] * tile(est_ref, t)
        copies.append(pltpu.make_async_copy(out_ref.at[:, spot], out_hbm.at[:, spot], sems.at[t]))
        copies[t].start()
    for copy in copies:
        copy.wait()


def swap_groups(tiles):
    group = lax.broadcasted_iota(jnp.int32, (8, 128), 1) // 16
    tiles = [tiles[0]] + [pltpu.roll(tiles[i], 16 * i, 1) for i in range(1, 8)]
    for b in (1, 2, 4):
        taken = (group & b) != 0
        tiles = [jnp.where(taken, tiles[(i + b) % 8], tiles[i]) for i in range(8)]
    return [tiles[0]] + [pltpu.roll(tiles[8 - i], 128 - 16 * i, 1) for i in range(1, 8)]


def unpack_one(in_ref, out_ref, rows_ref, per, offset):
    for zc in range(8):
        for half in range(2):
            at = zc * 8 * per + half * 8 + offset
            tiles = swap_groups([in_ref[at + per * i : at + per * i + 8, :] for i in range(8)])
            at = zc * 128 + half * 8
            for i in range(8):
                rows_ref[at + 16 * i : at + 16 * i + 8, :] = tiles[i]
    for zc in range(8):
        for x in range(16):
            out_ref[x, zc * 8 : zc * 8 + 8, :] = rows_ref[pl.ds(zc * 128 + x, 8, stride=16), :]


def unpack_kernel(in_hbm, out_ref, in_ref, rows_ref, sem):
    copy = pltpu.make_async_copy(in_hbm, in_ref, sem)
    copy.start()
    copy.wait()
    unpack_one(in_ref, out_ref, rows_ref, 16, 0)


def arrive_kernel(in_ref, y_ref, up_ref, down_ref, rows_ref, more_ref, obs_ref):
    unpack_one(in_ref, up_ref, rows_ref, 32, 0)
    unpack_one(in_ref, obs_ref, more_ref, 32, 16)
    y = split(y_ref[...])
    for x in range(16):
        v = dot(split(up_ref[x, :64, :]), y)
        up_ref[x, :64, :] = v
        down_ref[x, :64, :] = v
        up_ref[x, 64:, :] = obs_ref[x, 32:, :]
        down_ref[x, 64:, :] = obs_ref[x, :32, :]


def pack_one(in_ref, out_ref, rows_ref, per, offset):
    for zc in range(8):
        for x in range(16):
            rows_ref[pl.ds(zc * 128 + x, 8, stride=16), :] = in_ref[x, zc * 8 : zc * 8 + 8, :]
    for zc in range(8):
        for half in range(2):
            at = zc * 128 + half * 8
            tiles = swap_groups([rows_ref[at + 16 * i : at + 16 * i + 8, :] for i in range(8)])
            at = zc * 8 * per + half * 8 + offset
            for i in range(8):
                out_ref[at + per * i : at + per * i + 8, :] = tiles[i]


def exchange(rows):
    per = rows.shape[0] // 64
    t = lax.all_to_all(rows.reshape(64, per, 128), SLAB, 0, 0, tiled=True)
    return t.reshape(rows.shape)


def tap_vectors(psf_ref, flip):
    total = psf_ref[0]
    for k in range(1, 31):
        total = total + psf_ref[k]
    scale = 1.0 / jnp.full((8, 128), total, jnp.float32)
    return [psf_ref[30 - k if flip else k] * scale for k in range(31)]


def add_block(w, ref, z, acc, shift):
    for j in range(16):
        v = ref[j, z, :]
        for i in range(16):
            k = j + shift - i + 15
            if 0 <= k <= 30:
                p = w[k] * v
                acc[i] = p if acc[i] is None else acc[i] + p
    return acc


def over_planes(body):
    def step(t, _):
        body(pl.ds(pl.multiple_of(t * 8, 8), 8))
        return 0

    lax.fori_loop(0, 8, step, 0)


def own_x_kernel(flip, psf_ref, own_ref, out_ref):
    w = tap_vectors(psf_ref, flip)

    def body(z):
        acc = add_block(w, own_ref, z, [None] * 16, 0)
        for i in range(16):
            out_ref[i, z, :] = acc[i]

    over_planes(body)


def add_sides(w, core_ref, part_ref, passed_ref, swapped_ref, finish):
    def run(shift):
        def body(z):
            acc = [part_ref[i, z, :] for i in range(16)]
            acc = add_block(w, swapped_ref, z, acc, shift)
            finish(z, add_block(w, passed_ref, z, acc, -shift))

        over_planes(body)

    pl.when(core_ref[0] == 0)(lambda: run(16))
    pl.when(core_ref[0] != 0)(lambda: run(-16))


def sides_kernel(flip, psf_ref, core_ref, swapped_ref, passed_ref, part_ref, out_ref):
    def finish(z, acc):
        for i in range(16):
            out_ref[i, z, :] = acc[i]

    add_sides(tap_vectors(psf_ref, flip), core_ref, part_ref, passed_ref, swapped_ref, finish)


def update_kernel(
    flip, psf_ref, core_ref, swapped_ref, passed_ref, part_ref, est_ref, y_ref, rows_ref, out_ref,
    new_ref, turn_ref
):
    def finish(z, acc):
        for i in range(16):
            new_ref[i, z, :] = est_ref[i, z, :] * acc[i]

    add_sides(tap_vectors(psf_ref, flip), core_ref, part_ref, passed_ref, swapped_ref, finish)
    y = split(y_ref[...])
    for i in range(16):
        out_ref[i] = dot(split(new_ref[i]), y)
    pack_one(new_ref, rows_ref, turn_ref, 16, 0)


def x_halo(v, psf, flip, later):
    passed = lax.ppermute(v, SLAB, NEXT)
    swapped = lax.ppermute(v, "c", SWAP)
    part = call(functools.partial(own_x_kernel, flip), BLOCK, [psf, v], 1.3, "x_own")
    later, part = lax.optimization_barrier((later, part))
    return [swapped, passed, part], later


def high_planes(slab_ref, v_ref, above_ref, obs, mats, sum_ref, low_ref):
    has_above = jnp.full((32, 128), slab_ref[0], jnp.int32) < 7
    own, band, adjoint = [split(m[...]) for m in mats]
    for x in range(16):
        part = dot(own, split(v_ref[x, :64, :]))
        low_ref[x] = part[:64]
        sum_ref[x] = part[64:] + dot(band, split(above_ref[x, :64, :]))
    for x in range(16):
        sum_ref[x, :32, :] = obs(2, x) / sum_ref[x, :32, :]
        sum_ref[x, 32:, :] = jnp.where(has_above, obs(3, x) / sum_ref[x, 32:, :], 0.0)
    for x in range(16):
        sum_ref[x] = dot(adjoint, split(sum_ref[x]))


def low_planes(slab_ref, low_ref, sum_ref, below_ref, obs, mats, out_ref):
    has_below = jnp.full((32, 128), slab_ref[0], jnp.int32) > 0
    band, adjoint, y = [split(m[...]) for m in mats]
    for x in range(16):
        out_ref[x] = low_ref[x] + dot(band, split(below_ref[x, :64, :]))
    for x in range(16):
        out_ref[x, :32, :] = jnp.where(has_below, obs(0, x) / out_ref[x, :32, :], 0.0)
        out_ref[x, 32:, :] = obs(1, x) / out_ref[x, 32:, :]
    for x in range(16):
        out_ref[x] = sum_ref[x] + dot(adjoint, split(out_ref[x]))
    for x in range(16):
        out_ref[x] = dot(split(out_ref[x]), y)


def first_high_kernel(slab_ref, up_ref, above_ref, zo_ref, zh_ref, ah_ref, *refs):
    sum_ref, low_ref, halo_hbm, sems = refs
    copies = save_observed([above_ref], halo_hbm, sems)

    def obs(i, x):
        return (up_ref, above_ref)[i - 2][x, 64:, :]

    high_planes(slab_ref, up_ref, above_ref, obs, (zo_ref, zh_ref, ah_ref), sum_ref, low_ref)
    for copy in copies:
        copy.wait()


def first_low_kernel(slab_ref, low_ref, sum_ref, down_ref, below_ref, zl_ref, al_ref, ya_ref, *refs):
    out_ref, halo_hbm, sems = refs
    copies = save_observed([below_ref], halo_hbm, sems)

    def obs(i, x):
        return (below_ref, down_ref)[i][x, 64:, :]

    low_planes(slab_ref, low_ref, sum_ref, below_ref, obs, (zl_ref, al_ref, ya_ref), out_ref)
    for copy in copies:
        copy.wait()


def high_kernel(
    slab_ref, v_ref, above_ref, halo_ref, obs_ref, zo_ref, zh_ref, ah_ref, sum_ref, low_ref
):
    def obs(i, x):
        return obs_ref[x, 32:, :] if i == 2 else halo_ref[x]

    high_planes(slab_ref, v_ref, above_ref, obs, (zo_ref, zh_ref, ah_ref), sum_ref, low_ref)


def low_kernel(
    slab_ref, low_ref, sum_ref, below_ref, obs_ref, halo_ref, zl_ref, al_ref, ya_ref,
    out_ref, back_ref, rows_ref
):
    def obs(i, x):
        return obs_ref[x, :32, :] if i else halo_ref[x]

    low_planes(slab_ref, low_ref, sum_ref, below_ref, obs, (zl_ref, al_ref, ya_ref), back_ref)
    pack_one(back_ref, out_ref, rows_ref, 16, 0)


def per_device(observed, estimate, psf_y, psf_x, psf_z):
    core = lax.axis_index("c").reshape(1)
    slab = lax.axis_index("z").reshape(1)
    est0, obs0 = estimate.reshape(128, 1024), observed.reshape(128, 1024)

    first = pl.pallas_call(
        first_kernel,
        out_shape=pltpu.VMEM((2048, 128), jnp.float32),
        in_specs=[HBM, HBM, HBM],
        out_specs=VMEM,
        scratch_shapes=[
            pltpu.VMEM((128, 1024), jnp.float32),
            pltpu.VMEM((128, 1024), jnp.float32),
            pltpu.SMEM((31,), jnp.float32),
            pltpu.SemaphoreType.DMA((17,)),
        ],
        compiler_params=pltpu.CompilerParams(vmem_limit_bytes=LIMIT),
        name="first",
    )(*[pltpu.with_memory_space_constraint(a, pltpu.HBM) for a in (psf_x, est0, obs0)])
    arrived = exchange(first)
    yf, ya, xn, xf, zo, zl, zh, al, ah = prepare(psf_y, psf_x, psf_z)
    low_mats, high_mats = [zl, al, ya], [zo, zh, ah]
    halo = (16, 32, 128)
    out = [(16, 96, 128), (16, 96, 128)]
    up, down = call(arrive_kernel, out, [arrived, yf], 2, "arrive", [ROWS, ROWS, BLOCK])
    below = lax.ppermute(up, "z", UP)
    above = lax.ppermute(down, "z", DOWN)
    turned, obs = call(turn_kernel, ROWS, [est0, down, up], 1, "turn", save=BLOCK)
    rode = exchange(turned)
    args = [slab, up, above, *high_mats]
    total, low, halo_above = call(
        first_high_kernel, [BLOCK, BLOCK], args, 1, "first_high", save=halo
    )
    args = [slab, low, total, down, below, *low_mats]
    back, halo_below = call(first_low_kernel, BLOCK, args, 100, "first_low", save=halo)
    est = pl.pallas_call(
        unpack_kernel,
        out_shape=pltpu.VMEM(BLOCK, jnp.float32),
        in_specs=[HBM],
        out_specs=VMEM,
        scratch_shapes=[
            pltpu.VMEM(ROWS, jnp.float32),
            pltpu.VMEM(ROWS, jnp.float32),
            pltpu.SemaphoreType.DMA(()),
        ],
        cost_estimate=pl.CostEstimate(flops=10**9, bytes_accessed=10**6, transcendentals=0),
        compiler_params=pltpu.CompilerParams(vmem_limit_bytes=LIMIT),
        name="unpack",
    )(pltpu.with_memory_space_constraint(rode, pltpu.HBM))
    sides, _ = x_halo(back, psf_x, True, ())
    est_rows, v = call(
        functools.partial(update_kernel, True),
        [ROWS, BLOCK],
        [psf_x, core, *sides, est, yf],
        2,
        "update",
        [BLOCK, ROWS],
    )
    sides, est_rows = x_halo(v, psf_x, False, est_rows)
    est_rows = exchange(est_rows)
    v = call(functools.partial(sides_kernel, False), BLOCK, [psf_x, core, *sides], 1, "x_sides")

    below = lax.ppermute(v, "z", UP)
    above = lax.ppermute(v, "z", DOWN)
    args = [slab, v, above, halo_above, obs, *high_mats]
    total, low = call(high_kernel, [BLOCK, BLOCK], args, 1, "ratio_high")
    args = [slab, low, total, below, obs, halo_below, *low_mats]
    rows = call(low_kernel, ROWS, args, 4, "ratio_low", [BLOCK, ROWS])
    rows = exchange(rows)
    out = pl.pallas_call(
        last_kernel,
        out_shape=pltpu.HBM((128, 1024), jnp.float32),
        in_specs=[VMEM] * 4,
        out_specs=HBM,
        scratch_shapes=[pltpu.VMEM((128, 1024), jnp.float32), pltpu.SemaphoreType.DMA((8,))],
        compiler_params=pltpu.CompilerParams(vmem_limit_bytes=LIMIT),
        name="last",
    )(*[pltpu.with_memory_space_constraint(a, pltpu.VMEM) for a in (rows, est_rows, xn, xf)])
    return out.reshape(8, 16, 1024)


def solution(mesh):
    fine = Mesh(mesh.devices.reshape(8, 4, 2, 4, 2), ("z", "x", "yl", "yh", "c"))
    spec = P(("z", "x", "yl"), ("yh", "c"), None)
    return jax.shard_map(
        per_device,
        mesh=fine,
        in_specs=(spec, spec, P(), P(), P()),
        out_specs=spec,
        check_vma=False,
    )
```

```python
import functools

import jax
import jax.numpy as jnp
from jax import lax
from jax.experimental import pallas as pl
from jax.experimental.pallas import tpu as pltpu
from jax.sharding import Mesh, PartitionSpec as P

LIMIT = 6 * 2**20
SLAB = ("x", "yl", "yh", "c")
BLOCK = (16, 64, 128)
ROWS = (1024, 128)
VMEM = pl.BlockSpec(memory_space=pltpu.VMEM)
SMEM = pl.BlockSpec(memory_space=pltpu.SMEM)
HBM = pl.BlockSpec(memory_space=pltpu.HBM)


def x_index(b, c):
    x, yh, yl = b // 8, (b % 8) // 2, b % 2
    return ((x * 2 + yl) * 4 + yh) * 2 + c


SWAP = [(0, 1), (1, 0)]
NEXT = [(x_index(b, 0), x_index(b - 1, 1)) for b in range(1, 32)] + [
    (x_index(b, 1), x_index(b + 1, 0)) for b in range(31)
]
UP = [(z, z + 1) for z in range(7)]
DOWN = [(z + 1, z) for z in range(7)]


def is_shape(s):
    return isinstance(s, tuple)


def call(kernel, out, args, us, name, scratch=(), save=None):
    args = [a if a.ndim == 1 else pltpu.with_memory_space_constraint(a, pltpu.VMEM) for a in args]
    shapes = jax.tree.map(lambda s: pltpu.VMEM(s, jnp.float32), out, is_leaf=is_shape)
    specs = jax.tree.map(lambda s: VMEM, out, is_leaf=is_shape)
    scratch = [pltpu.VMEM(s, jnp.float32) for s in scratch]
    if save:
        shapes = [*(shapes if isinstance(shapes, list) else [shapes]), pltpu.HBM(save, jnp.float32)]
        specs = [*(specs if isinstance(specs, list) else [specs]), HBM]
        scratch.append(pltpu.SemaphoreType.DMA((2,)))
    return pl.pallas_call(
        kernel,
        out_shape=shapes,
        in_specs=[SMEM if a.ndim == 1 else VMEM for a in args],
        out_specs=specs,
        scratch_shapes=scratch,
        cost_estimate=pl.CostEstimate(
            flops=int(us * 1e9), bytes_accessed=int(us * 3e6), transcendentals=0
        ),
        compiler_params=pltpu.CompilerParams(vmem_limit_bytes=LIMIT),
        name=name,
    )(*args)


def split(m):
    high = m.astype(jnp.bfloat16)
    return high, (m - high.astype(jnp.float32)).astype(jnp.bfloat16)


def dot(a, b):
    (ah, al), (bh, bl) = a, b

    def one(p, q):
        return jnp.dot(p, q, preferred_element_type=jnp.float32)

    return one(ah, bh) + (one(al, bh) + one(ah, bl))


def band(psf_ref, lead, flip, rows):
    taps = psf_ref.shape[0]
    lane = lax.broadcasted_iota(jnp.int32, (8, 256), 1)
    line = jnp.zeros((8, 256), jnp.float32)
    total = psf_ref[0]
    for k in range(taps):
        if k:
            total = total + psf_ref[k]
        line = jnp.where(lane == (k + lead) % 256, psf_ref[taps - 1 - k if flip else k], line)
    line = line / jnp.full((8, 256), total, jnp.float32)
    return pltpu.roll(jnp.broadcast_to(line[:1], (rows, 256)), 0, 1, stride=1, stride_axis=0)


def x_band(psf_ref, flip):
    m = band(psf_ref, -15, not flip, 128)
    return m[:, :128], m[:, 128:]


def prep_kernel(
    psf_y_ref, psf_x_ref, psf_z_ref, yf_ref, ya_ref, xn_ref, xf_ref, zo_ref, zl_ref, zh_ref, al_ref, ah_ref
):
    yf_ref[...] = band(psf_y_ref, -15, True, 128)[:, :128]
    ya_ref[...] = band(psf_y_ref, -15, False, 128)[:, :128]
    xn_ref[...], xf_ref[...] = x_band(psf_x_ref, True)
    fwd = band(psf_z_ref, 1, False, 128)
    zl_ref[...] = fwd[:64, :64]
    zo_ref[...] = fwd[:, 64:128]
    zh_ref[...] = fwd[64:, 128:192]
    adjoint = band(psf_z_ref, 1, True, 64)
    al_ref[...], ah_ref[...] = adjoint[:, :64], adjoint[:, 64:128]


def prepare(psf_y, psf_x, psf_z):
    out = [(128, 128)] * 4 + [(128, 64)] + [(64, 64)] * 4
    return call(prep_kernel, out, [psf_y, psf_x, psf_z], 1, "prepare")


def blur_lanes(tiles, near, far):
    lane = lax.broadcasted_iota(jnp.int32, tiles[0].shape, 1)
    zero = jnp.zeros_like(tiles[0])
    near, far = split(near), split(far)
    out = []
    for t in range(8):
        after = tiles[t + 1] if t < 7 else zero
        before = tiles[t - 1] if t > 0 else zero
        out.append(dot(split(tiles[t]), near) + dot(split(jnp.where(lane < 64, after, before)), far))
    return out


def rows_at(t, i, per=16, offset=0):
    block = 8 * t + i
    return x_index(block // 2, block % 2) * per + offset


def write_columns(out_ref, t, tile, per=16, offset=0):
    turned = tile.T
    for i in range(8):
        at = rows_at(t, i, per, offset)
        out_ref[at : at + 16, :] = turned[16 * i : 16 * i + 16, :]


def first_kernel(psf_x_hbm, est_hbm, obs_hbm, out_ref, est_ref, obs_ref, psf_x_ref, sems):
    taps = pltpu.make_async_copy(psf_x_hbm, psf_x_ref, sems.at[16])
    taps.start()
    copies = []
    for n, (src, dst) in enumerate(((est_hbm, est_ref), (obs_hbm, obs_ref))):
        for t in range(8):
            spot = pl.ds(128 * t, 128)
            copies.append(
                pltpu.make_async_copy(src.at[:, spot], dst.at[:, spot], sems.at[8 * n + t])
            )
            copies[-1].start()
    taps.wait()
    near, far = x_band(psf_x_ref, False)
    for copy in copies[:8]:
        copy.wait()
    blurred = blur_lanes([est_ref[:, 128 * t : 128 * t + 128] for t in range(8)], near, far)
    for t in range(8):
        write_columns(out_ref, t, blurred[t], 32, 0)
    for t in range(8):
        copies[8 + t].wait()
        write_columns(out_ref, t, obs_ref[:, 128 * t : 128 * t + 128], 32, 16)


def save_observed(refs, out_hbm, sems):
    copies = [
        pltpu.make_async_copy(
            ref.at[:, pl.ds(64, 32), :], out_hbm.at[:, pl.ds(32 * i, 32), :], sems.at[i]
        )
        for i, ref in enumerate(refs)
    ]
    for copy in copies:
        copy.start()
    return copies


def turn_kernel(in_ref, down_ref, up_ref, out_ref, obs_hbm, sems):
    copies = save_observed([down_ref, up_ref], obs_hbm, sems)
    for t in range(8):
        write_columns(out_ref, t, in_ref[:, 128 * t : 128 * t + 128])
    for copy in copies:
        copy.wait()


def last_kernel(back_ref, est_ref, near_ref, far_ref, out_hbm, out_ref, sems):
    def tile(ref, t):
        spots = [rows_at(t, i) for i in range(8)]
        return jnp.concatenate([ref[at : at + 16, :] for at in spots], axis=0).T

    blurred = blur_lanes([tile(back_ref, t) for t in range(8)], near_ref[...], far_ref[...])
    copies = []
    for t in range(8):
        spot = pl.ds(128 * t, 128)
        out_ref[:, spot] = blurred[t] * tile(est_ref, t)
        copies.append(pltpu.make_async_copy(out_ref.at[:, spot], out_hbm.at[:, spot], sems.at[t]))
        copies[t].start()
    for copy in copies:
        copy.wait()


def swap_groups(tiles):
    group = lax.broadcasted_iota(jnp.int32, (8, 128), 1) // 16
    tiles = [tiles[0]] + [pltpu.roll(tiles[i], 16 * i, 1) for i in range(1, 8)]
    for b in (1, 2, 4):
        taken = (group & b) != 0
        tiles = [jnp.where(taken, tiles[(i + b) % 8], tiles[i]) for i in range(8)]
    return [tiles[0]] + [pltpu.roll(tiles[8 - i], 128 - 16 * i, 1) for i in range(1, 8)]


def unpack_one(in_ref, out_ref, rows_ref, per, offset):
    for zc in range(8):
        for half in range(2):
            at = zc * 8 * per + half * 8 + offset
            tiles = swap_groups([in_ref[at + per * i : at + per * i + 8, :] for i in range(8)])
            at = zc * 128 + half * 8
            for i in range(8):
                rows_ref[at + 16 * i : at + 16 * i + 8, :] = tiles[i]
    for zc in range(8):
        for x in range(16):
            out_ref[x, zc * 8 : zc * 8 + 8, :] = rows_ref[pl.ds(zc * 128 + x, 8, stride=16), :]


def unpack_kernel(in_hbm, out_ref, in_ref, rows_ref, sem):
    copy = pltpu.make_async_copy(in_hbm, in_ref, sem)
    copy.start()
    copy.wait()
    unpack_one(in_ref, out_ref, rows_ref, 16, 0)


def arrive_kernel(in_ref, y_ref, up_ref, down_ref, rows_ref, more_ref, obs_ref):
    unpack_one(in_ref, up_ref, rows_ref, 32, 0)
    unpack_one(in_ref, obs_ref, more_ref, 32, 16)
    y = split(y_ref[...])
    for x in range(16):
        v = dot(split(up_ref[x, :64, :]), y)
        up_ref[x, :64, :] = v
        down_ref[x, :64, :] = v
        up_ref[x, 64:, :] = obs_ref[x, 32:, :]
        down_ref[x, 64:, :] = obs_ref[x, :32, :]


def pack_one(in_ref, out_ref, rows_ref, per, offset):
    for zc in range(8):
        for x in range(16):
            rows_ref[pl.ds(zc * 128 + x, 8, stride=16), :] = in_ref[x, zc * 8 : zc * 8 + 8, :]
    for zc in range(8):
        for half in range(2):
            at = zc * 128 + half * 8
            tiles = swap_groups([rows_ref[at + 16 * i : at + 16 * i + 8, :] for i in range(8)])
            at = zc * 8 * per + half * 8 + offset
            for i in range(8):
                out_ref[at + per * i : at + per * i + 8, :] = tiles[i]


def exchange(rows):
    per = rows.shape[0] // 64
    t = lax.all_to_all(rows.reshape(64, per, 128), SLAB, 0, 0, tiled=True)
    return t.reshape(rows.shape)


def tap_vectors(psf_ref, flip):
    total = psf_ref[0]
    for k in range(1, 31):
        total = total + psf_ref[k]
    scale = 1.0 / jnp.full((8, 128), total, jnp.float32)
    return [psf_ref[30 - k if flip else k] * scale for k in range(31)]


def add_block(w, ref, z, acc, shift):
    for j in range(16):
        v = ref[j, z, :]
        for i in range(16):
            k = j + shift - i + 15
            if 0 <= k <= 30:
                p = w[k] * v
                acc[i] = p if acc[i] is None else acc[i] + p
    return acc


def over_planes(body):
    def step(t, _):
        body(pl.ds(pl.multiple_of(t * 8, 8), 8))
        return 0

    lax.fori_loop(0, 8, step, 0)


def own_x_kernel(flip, psf_ref, own_ref, out_ref):
    w = tap_vectors(psf_ref, flip)

    def body(z):
        acc = add_block(w, own_ref, z, [None] * 16, 0)
        for i in range(16):
            out_ref[i, z, :] = acc[i]

    over_planes(body)


def add_sides(w, core_ref, start, passed_ref, swapped_ref, finish):
    def run(shift):
        def body(z):
            acc = start(z)
            acc = add_block(w, swapped_ref, z, acc, shift)
            finish(z, add_block(w, passed_ref, z, acc, -shift))

        over_planes(body)

    pl.when(core_ref[0] == 0)(lambda: run(16))
    pl.when(core_ref[0] != 0)(lambda: run(-16))


def x_kernel(flip, psf_ref, core_ref, swapped_ref, passed_ref, own_ref, out_ref):
    w = tap_vectors(psf_ref, flip)

    def start(z):
        return add_block(w, own_ref, z, [None] * 16, 0)

    def finish(z, acc):
        for i in range(16):
            out_ref[i, z, :] = acc[i]

    add_sides(w, core_ref, start, passed_ref, swapped_ref, finish)


def update_kernel(
    flip, psf_ref, core_ref, swapped_ref, passed_ref, part_ref, est_ref, y_ref, rows_ref, out_ref,
    new_ref, turn_ref
):
    def finish(z, acc):
        for i in range(16):
            new_ref[i, z, :] = est_ref[i, z, :] * acc[i]

    def start(z):
        return [part_ref[i, z, :] for i in range(16)]

    w = tap_vectors(psf_ref, flip)
    add_sides(w, core_ref, start, passed_ref, swapped_ref, finish)
    y = split(y_ref[...])
    for i in range(16):
        out_ref[i] = dot(split(new_ref[i]), y)
    pack_one(new_ref, rows_ref, turn_ref, 16, 0)


def x_halo(v):
    swapped = lax.ppermute(v, "c", SWAP)
    passed = lax.ppermute(v, SLAB, NEXT)
    return [swapped, passed]


def high_planes(slab_ref, v_ref, above_ref, obs, mats, sum_ref, low_ref):
    has_above = jnp.full((32, 128), slab_ref[0], jnp.int32) < 7
    own, band, adjoint = [split(m[...]) for m in mats]
    for x in range(16):
        part = dot(own, split(v_ref[x, :64, :]))
        low_ref[x] = part[:64]
        sum_ref[x] = part[64:] + dot(band, split(above_ref[x, :64, :]))
    for x in range(16):
        sum_ref[x, :32, :] = obs(2, x) / sum_ref[x, :32, :]
        sum_ref[x, 32:, :] = jnp.where(has_above, obs(3, x) / sum_ref[x, 32:, :], 0.0)
    for x in range(16):
        sum_ref[x] = dot(adjoint, split(sum_ref[x]))


def low_planes(slab_ref, low_ref, sum_ref, below_ref, obs, mats, out_ref):
    has_below = jnp.full((32, 128), slab_ref[0], jnp.int32) > 0
    band, adjoint, y = [split(m[...]) for m in mats]
    for x in range(16):
        out_ref[x] = low_ref[x] + dot(band, split(below_ref[x, :64, :]))
    for x in range(16):
        out_ref[x, :32, :] = jnp.where(has_below, obs(0, x) / out_ref[x, :32, :], 0.0)
        out_ref[x, 32:, :] = obs(1, x) / out_ref[x, 32:, :]
    for x in range(16):
        out_ref[x] = sum_ref[x] + dot(adjoint, split(out_ref[x]))
    for x in range(16):
        out_ref[x] = dot(split(out_ref[x]), y)


def first_high_kernel(slab_ref, up_ref, above_ref, zo_ref, zh_ref, ah_ref, *refs):
    sum_ref, low_ref, halo_hbm, sems = refs
    copies = save_observed([above_ref], halo_hbm, sems)

    def obs(i, x):
        return (up_ref, above_ref)[i - 2][x, 64:, :]

    high_planes(slab_ref, up_ref, above_ref, obs, (zo_ref, zh_ref, ah_ref), sum_ref, low_ref)
    for copy in copies:
        copy.wait()


def first_low_kernel(slab_ref, low_ref, sum_ref, down_ref, below_ref, zl_ref, al_ref, ya_ref, *refs):
    out_ref, halo_hbm, sems = refs
    copies = save_observed([below_ref], halo_hbm, sems)

    def obs(i, x):
        return (below_ref, down_ref)[i][x, 64:, :]

    low_planes(slab_ref, low_ref, sum_ref, below_ref, obs, (zl_ref, al_ref, ya_ref), out_ref)
    for copy in copies:
        copy.wait()


def high_kernel(
    slab_ref, v_ref, above_ref, halo_ref, obs_ref, zo_ref, zh_ref, ah_ref, sum_ref, low_ref
):
    def obs(i, x):
        return obs_ref[x, 32:, :] if i == 2 else halo_ref[x]

    high_planes(slab_ref, v_ref, above_ref, obs, (zo_ref, zh_ref, ah_ref), sum_ref, low_ref)


def low_kernel(
    slab_ref, low_ref, sum_ref, below_ref, obs_ref, halo_ref, zl_ref, al_ref, ya_ref,
    out_ref, back_ref, rows_ref
):
    def obs(i, x):
        return obs_ref[x, :32, :] if i else halo_ref[x]

    low_planes(slab_ref, low_ref, sum_ref, below_ref, obs, (zl_ref, al_ref, ya_ref), back_ref)
    pack_one(back_ref, out_ref, rows_ref, 16, 0)


def per_device(observed, estimate, psf_y, psf_x, psf_z):
    core = lax.axis_index("c").reshape(1)
    slab = lax.axis_index("z").reshape(1)
    est0, obs0 = estimate.reshape(128, 1024), observed.reshape(128, 1024)

    first = pl.pallas_call(
        first_kernel,
        out_shape=pltpu.VMEM((2048, 128), jnp.float32),
        in_specs=[HBM, HBM, HBM],
        out_specs=VMEM,
        scratch_shapes=[
            pltpu.VMEM((128, 1024), jnp.float32),
            pltpu.VMEM((128, 1024), jnp.float32),
            pltpu.SMEM((31,), jnp.float32),
            pltpu.SemaphoreType.DMA((17,)),
        ],
        compiler_params=pltpu.CompilerParams(vmem_limit_bytes=LIMIT),
        name="first",
    )(*[pltpu.with_memory_space_constraint(a, pltpu.HBM) for a in (psf_x, est0, obs0)])
    arrived = exchange(first)
    yf, ya, xn, xf, zo, zl, zh, al, ah = prepare(psf_y, psf_x, psf_z)
    low_mats, high_mats = [zl, al, ya], [zo, zh, ah]
    halo = (16, 32, 128)
    out = [(16, 96, 128), (16, 96, 128)]
    up, down = call(arrive_kernel, out, [arrived, yf], 2, "arrive", [ROWS, ROWS, BLOCK])
    below = lax.ppermute(up, "z", UP)
    above = lax.ppermute(down, "z", DOWN)
    turned, obs = call(turn_kernel, ROWS, [est0, down, up], 1, "turn", save=BLOCK)
    rode = exchange(turned)
    args = [slab, up, above, *high_mats]
    total, low, halo_above = call(
        first_high_kernel, [BLOCK, BLOCK], args, 1, "first_high", save=halo
    )
    args = [slab, low, total, down, below, *low_mats]
    back, halo_below = call(first_low_kernel, BLOCK, args, 100, "first_low", save=halo)
    est = pl.pallas_call(
        unpack_kernel,
        out_shape=pltpu.VMEM(BLOCK, jnp.float32),
        in_specs=[HBM],
        out_specs=VMEM,
        scratch_shapes=[
            pltpu.VMEM(ROWS, jnp.float32),
            pltpu.VMEM(ROWS, jnp.float32),
            pltpu.SemaphoreType.DMA(()),
        ],
        cost_estimate=pl.CostEstimate(flops=10**9, bytes_accessed=10**6, transcendentals=0),
        compiler_params=pltpu.CompilerParams(vmem_limit_bytes=LIMIT),
        name="unpack",
    )(pltpu.with_memory_space_constraint(rode, pltpu.HBM))
    part = call(functools.partial(own_x_kernel, True), BLOCK, [psf_x, back], 1.3, "x_own")
    sides = [*x_halo(back), part]
    est_rows, v = call(
        functools.partial(update_kernel, True),
        [ROWS, BLOCK],
        [psf_x, core, *sides, est, yf],
        2,
        "update",
        [BLOCK, ROWS],
    )
    args = [psf_x, core, *x_halo(v), v]
    est_rows = exchange(est_rows)
    v = call(functools.partial(x_kernel, False), BLOCK, args, 100, "x_all")

    below = lax.ppermute(v, "z", UP)
    above = lax.ppermute(v, "z", DOWN)
    args = [slab, v, above, halo_above, obs, *high_mats]
    total, low = call(high_kernel, [BLOCK, BLOCK], args, 1, "ratio_high")
    args = [slab, low, total, below, obs, halo_below, *low_mats]
    rows = call(low_kernel, ROWS, args, 4, "ratio_low", [BLOCK, ROWS])
    rows = exchange(rows)
    out = pl.pallas_call(
        last_kernel,
        out_shape=pltpu.HBM((128, 1024), jnp.float32),
        in_specs=[VMEM] * 4,
        out_specs=HBM,
        scratch_shapes=[pltpu.VMEM((128, 1024), jnp.float32), pltpu.SemaphoreType.DMA((8,))],
        compiler_params=pltpu.CompilerParams(vmem_limit_bytes=LIMIT),
        name="last",
    )(*[pltpu.with_memory_space_constraint(a, pltpu.VMEM) for a in (rows, est_rows, xn, xf)])
    return out.reshape(8, 16, 1024)


def solution(mesh):
    fine = Mesh(mesh.devices.reshape(8, 4, 2, 4, 2), ("z", "x", "yl", "yh", "c"))
    spec = P(("z", "x", "yl"), ("yh", "c"), None)
    return jax.shard_map(
        per_device,
        mesh=fine,
        in_specs=(spec, spec, P(), P(), P()),
        out_specs=spec,
        check_vma=False,
    )
```

```python
import functools

import jax
import jax.numpy as jnp
from jax import lax
from jax.experimental import pallas as pl
from jax.experimental.pallas import tpu as pltpu
from jax.sharding import Mesh, PartitionSpec as P

LIMIT = 6 * 2**20
SLAB = ("x", "yl", "yh", "c")
BLOCK = (16, 64, 128)
ROWS = (1024, 128)
VMEM = pl.BlockSpec(memory_space=pltpu.VMEM)
SMEM = pl.BlockSpec(memory_space=pltpu.SMEM)
HBM = pl.BlockSpec(memory_space=pltpu.HBM)


def x_index(b, c):
    x, yh, yl = b // 8, (b % 8) // 2, b % 2
    return ((x * 2 + yl) * 4 + yh) * 2 + c


SWAP = [(0, 1), (1, 0)]
NEXT = [(x_index(b, 0), x_index(b - 1, 1)) for b in range(1, 32)] + [
    (x_index(b, 1), x_index(b + 1, 0)) for b in range(31)
]
UP = [(z, z + 1) for z in range(7)]
DOWN = [(z + 1, z) for z in range(7)]


def is_shape(s):
    return isinstance(s, tuple)


def call(kernel, out, args, us, name, scratch=(), save=None):
    args = [a if a.ndim == 1 else pltpu.with_memory_space_constraint(a, pltpu.VMEM) for a in args]
    shapes = jax.tree.map(lambda s: pltpu.VMEM(s, jnp.float32), out, is_leaf=is_shape)
    specs = jax.tree.map(lambda s: VMEM, out, is_leaf=is_shape)
    scratch = [pltpu.VMEM(s, jnp.float32) for s in scratch]
    if save:
        shapes = [*(shapes if isinstance(shapes, list) else [shapes]), pltpu.HBM(save, jnp.float32)]
        specs = [*(specs if isinstance(specs, list) else [specs]), HBM]
        scratch.append(pltpu.SemaphoreType.DMA((2,)))
    return pl.pallas_call(
        kernel,
        out_shape=shapes,
        in_specs=[SMEM if a.ndim == 1 else VMEM for a in args],
        out_specs=specs,
        scratch_shapes=scratch,
        cost_estimate=pl.CostEstimate(
            flops=int(us * 1e9), bytes_accessed=int(us * 3e6), transcendentals=0
        ),
        compiler_params=pltpu.CompilerParams(vmem_limit_bytes=LIMIT),
        name=name,
    )(*args)


def split(m):
    high = m.astype(jnp.bfloat16)
    return high, (m - high.astype(jnp.float32)).astype(jnp.bfloat16)


def dot(a, b):
    (ah, al), (bh, bl) = a, b

    def one(p, q):
        return jnp.dot(p, q, preferred_element_type=jnp.float32)

    return one(ah, bh) + (one(al, bh) + one(ah, bl))


def band(psf_ref, lead, flip, rows):
    taps = psf_ref.shape[0]
    lane = lax.broadcasted_iota(jnp.int32, (8, 256), 1)
    line = jnp.zeros((8, 256), jnp.float32)
    total = psf_ref[0]
    for k in range(taps):
        if k:
            total = total + psf_ref[k]
        line = jnp.where(lane == (k + lead) % 256, psf_ref[taps - 1 - k if flip else k], line)
    line = line / jnp.full((8, 256), total, jnp.float32)
    return pltpu.roll(jnp.broadcast_to(line[:1], (rows, 256)), 0, 1, stride=1, stride_axis=0)


def x_band(psf_ref, flip):
    m = band(psf_ref, -15, not flip, 128)
    return m[:, :128], m[:, 128:]


def prep_kernel(
    psf_y_ref, psf_x_ref, psf_z_ref, yf_ref, ya_ref, xn_ref, xf_ref, zo_ref, zl_ref, zh_ref, al_ref, ah_ref
):
    yf_ref[...] = band(psf_y_ref, -15, True, 128)[:, :128]
    ya_ref[...] = band(psf_y_ref, -15, False, 128)[:, :128]
    xn_ref[...], xf_ref[...] = x_band(psf_x_ref, True)
    fwd = band(psf_z_ref, 1, False, 128)
    zl_ref[...] = fwd[:64, :64]
    zo_ref[...] = fwd[:, 64:128]
    zh_ref[...] = fwd[64:, 128:192]
    adjoint = band(psf_z_ref, 1, True, 64)
    al_ref[...], ah_ref[...] = adjoint[:, :64], adjoint[:, 64:128]


def prepare(psf_y, psf_x, psf_z):
    out = [(128, 128)] * 4 + [(128, 64)] + [(64, 64)] * 4
    return call(prep_kernel, out, [psf_y, psf_x, psf_z], 1, "prepare")


def blur_lanes(tiles, near, far):
    lane = lax.broadcasted_iota(jnp.int32, tiles[0].shape, 1)
    zero = jnp.zeros_like(tiles[0])
    near, far = split(near), split(far)
    out = []
    for t in range(8):
        after = tiles[t + 1] if t < 7 else zero
        before = tiles[t - 1] if t > 0 else zero
        out.append(dot(split(tiles[t]), near) + dot(split(jnp.where(lane < 64, after, before)), far))
    return out


def rows_at(t, i, per=16, offset=0):
    block = 8 * t + i
    return x_index(block // 2, block % 2) * per + offset


def write_columns(out_ref, t, tile, per=16, offset=0):
    turned = tile.T
    for i in range(8):
        at = rows_at(t, i, per, offset)
        out_ref[at : at + 16, :] = turned[16 * i : 16 * i + 16, :]


def first_kernel(psf_x_hbm, est_hbm, obs_hbm, out_ref, est_ref, obs_ref, psf_x_ref, sems):
    taps = pltpu.make_async_copy(psf_x_hbm, psf_x_ref, sems.at[16])
    taps.start()
    copies = [
        pltpu.make_async_copy(
            src.at[pl.ds(64 * i, 64), :], dst.at[pl.ds(64 * i, 64), :], sems.at[2 * n + i]
        )
        for n, (src, dst) in enumerate(((est_hbm, est_ref), (obs_hbm, obs_ref)))
        for i in range(2)
    ]
    for copy in copies:
        copy.start()
    taps.wait()
    near, far = x_band(psf_x_ref, False)
    copies[0].wait()
    copies[1].wait()
    blurred = blur_lanes([est_ref[:, 128 * t : 128 * t + 128] for t in range(8)], near, far)
    for t in range(8):
        write_columns(out_ref, t, blurred[t], 32, 0)
    copies[2].wait()
    copies[3].wait()
    for t in range(8):
        write_columns(out_ref, t, obs_ref[:, 128 * t : 128 * t + 128], 32, 16)


def save_observed(refs, out_hbm, sems):
    copies = [
        pltpu.make_async_copy(
            ref.at[:, pl.ds(64, 32), :], out_hbm.at[:, pl.ds(32 * i, 32), :], sems.at[i]
        )
        for i, ref in enumerate(refs)
    ]
    for copy in copies:
        copy.start()
    return copies


def turn_kernel(in_ref, down_ref, up_ref, out_ref, obs_hbm, sems):
    copies = save_observed([down_ref, up_ref], obs_hbm, sems)
    for t in range(8):
        write_columns(out_ref, t, in_ref[:, 128 * t : 128 * t + 128])
    for copy in copies:
        copy.wait()


def last_kernel(back_ref, est_ref, near_ref, far_ref, out_hbm, out_ref, sems):
    def tile(ref, t):
        spots = [rows_at(t, i) for i in range(8)]
        return jnp.concatenate([ref[at : at + 16, :] for at in spots], axis=0).T

    blurred = blur_lanes([tile(back_ref, t) for t in range(8)], near_ref[...], far_ref[...])
    copies = []
    for t in range(8):
        spot = pl.ds(128 * t, 128)
        out_ref[:, spot] = blurred[t] * tile(est_ref, t)
        copies.append(pltpu.make_async_copy(out_ref.at[:, spot], out_hbm.at[:, spot], sems.at[t]))
        copies[t].start()
    for copy in copies:
        copy.wait()


def swap_groups(tiles):
    group = lax.broadcasted_iota(jnp.int32, (8, 128), 1) // 16
    tiles = [tiles[0]] + [pltpu.roll(tiles[i], 16 * i, 1) for i in range(1, 8)]
    for b in (1, 2, 4):
        taken = (group & b) != 0
        tiles = [jnp.where(taken, tiles[(i + b) % 8], tiles[i]) for i in range(8)]
    return [tiles[0]] + [pltpu.roll(tiles[8 - i], 128 - 16 * i, 1) for i in range(1, 8)]


def unpack_one(in_ref, out_ref, rows_ref, per, offset):
    for zc in range(8):
        for half in range(2):
            at = zc * 8 * per + half * 8 + offset
            tiles = swap_groups([in_ref[at + per * i : at + per * i + 8, :] for i in range(8)])
            at = zc * 128 + half * 8
            for i in range(8):
                rows_ref[at + 16 * i : at + 16 * i + 8, :] = tiles[i]
    for zc in range(8):
        for x in range(16):
            out_ref[x, zc * 8 : zc * 8 + 8, :] = rows_ref[pl.ds(zc * 128 + x, 8, stride=16), :]


def unpack_kernel(in_hbm, out_ref, in_ref, rows_ref, sem):
    copy = pltpu.make_async_copy(in_hbm, in_ref, sem)
    copy.start()
    copy.wait()
    unpack_one(in_ref, out_ref, rows_ref, 16, 0)


def arrive_kernel(in_ref, y_ref, up_ref, down_ref, rows_ref, more_ref, obs_ref):
    unpack_one(in_ref, up_ref, rows_ref, 32, 0)
    unpack_one(in_ref, obs_ref, more_ref, 32, 16)
    y = split(y_ref[...])
    for x in range(16):
        v = dot(split(up_ref[x, :64, :]), y)
        up_ref[x, :64, :] = v
        down_ref[x, :64, :] = v
        up_ref[x, 64:, :] = obs_ref[x, 32:, :]
        down_ref[x, 64:, :] = obs_ref[x, :32, :]


def pack_one(in_ref, out_ref, rows_ref, per, offset):
    for zc in range(8):
        for x in range(16):
            rows_ref[pl.ds(zc * 128 + x, 8, stride=16), :] = in_ref[x, zc * 8 : zc * 8 + 8, :]
    for zc in range(8):
        for half in range(2):
            at = zc * 128 + half * 8
            tiles = swap_groups([rows_ref[at + 16 * i : at + 16 * i + 8, :] for i in range(8)])
            at = zc * 8 * per + half * 8 + offset
            for i in range(8):
                out_ref[at + per * i : at + per * i + 8, :] = tiles[i]


def exchange(rows):
    per = rows.shape[0] // 64
    t = lax.all_to_all(rows.reshape(64, per, 128), SLAB, 0, 0, tiled=True)
    return t.reshape(rows.shape)


def tap_vectors(psf_ref, flip):
    total = psf_ref[0]
    for k in range(1, 31):
        total = total + psf_ref[k]
    scale = 1.0 / jnp.full((8, 128), total, jnp.float32)
    return [psf_ref[30 - k if flip else k] * scale for k in range(31)]


def add_block(w, ref, z, acc, shift):
    for j in range(16):
        v = ref[j, z, :]
        for i in range(16):
            k = j + shift - i + 15
            if 0 <= k <= 30:
                p = w[k] * v
                acc[i] = p if acc[i] is None else acc[i] + p
    return acc


def over_planes(body):
    def step(t, _):
        body(pl.ds(pl.multiple_of(t * 8, 8), 8))
        return 0

    lax.fori_loop(0, 8, step, 0)


def own_x_kernel(flip, psf_ref, own_ref, out_ref):
    w = tap_vectors(psf_ref, flip)

    def body(z):
        acc = add_block(w, own_ref, z, [None] * 16, 0)
        for i in range(16):
            out_ref[i, z, :] = acc[i]

    over_planes(body)


def add_sides(w, core_ref, start, passed_ref, swapped_ref, finish):
    def run(shift):
        def body(z):
            acc = start(z)
            acc = add_block(w, swapped_ref, z, acc, shift)
            finish(z, add_block(w, passed_ref, z, acc, -shift))

        over_planes(body)

    pl.when(core_ref[0] == 0)(lambda: run(16))
    pl.when(core_ref[0] != 0)(lambda: run(-16))


def x_kernel(flip, psf_ref, core_ref, swapped_ref, passed_ref, own_ref, out_ref):
    w = tap_vectors(psf_ref, flip)

    def start(z):
        return add_block(w, own_ref, z, [None] * 16, 0)

    def finish(z, acc):
        for i in range(16):
            out_ref[i, z, :] = acc[i]

    add_sides(w, core_ref, start, passed_ref, swapped_ref, finish)


def update_kernel(
    flip, psf_ref, core_ref, swapped_ref, passed_ref, part_ref, est_ref, y_ref, rows_ref, out_ref,
    new_ref, turn_ref
):
    def finish(z, acc):
        for i in range(16):
            new_ref[i, z, :] = est_ref[i, z, :] * acc[i]

    def start(z):
        return [part_ref[i, z, :] for i in range(16)]

    w = tap_vectors(psf_ref, flip)
    add_sides(w, core_ref, start, passed_ref, swapped_ref, finish)
    y = split(y_ref[...])
    for i in range(16):
        out_ref[i] = dot(split(new_ref[i]), y)
    pack_one(new_ref, rows_ref, turn_ref, 16, 0)


def x_halo(v):
    swapped = lax.ppermute(v, "c", SWAP)
    passed = lax.ppermute(v, SLAB, NEXT)
    return [swapped, passed]


def high_planes(slab_ref, v_ref, above_ref, obs, mats, sum_ref, low_ref):
    has_above = jnp.full((32, 128), slab_ref[0], jnp.int32) < 7
    own, band, adjoint = [split(m[...]) for m in mats]
    for x in range(16):
        part = dot(own, split(v_ref[x, :64, :]))
        low_ref[x] = part[:64]
        sum_ref[x] = part[64:] + dot(band, split(above_ref[x, :64, :]))
    for x in range(16):
        sum_ref[x, :32, :] = obs(2, x) / sum_ref[x, :32, :]
        sum_ref[x, 32:, :] = jnp.where(has_above, obs(3, x) / sum_ref[x, 32:, :], 0.0)
    for x in range(16):
        sum_ref[x] = dot(adjoint, split(sum_ref[x]))


def low_planes(slab_ref, low_ref, sum_ref, below_ref, obs, mats, out_ref):
    has_below = jnp.full((32, 128), slab_ref[0], jnp.int32) > 0
    band, adjoint, y = [split(m[...]) for m in mats]
    for x in range(16):
        out_ref[x] = low_ref[x] + dot(band, split(below_ref[x, :64, :]))
    for x in range(16):
        out_ref[x, :32, :] = jnp.where(has_below, obs(0, x) / out_ref[x, :32, :], 0.0)
        out_ref[x, 32:, :] = obs(1, x) / out_ref[x, 32:, :]
    for x in range(16):
        out_ref[x] = sum_ref[x] + dot(adjoint, split(out_ref[x]))
    for x in range(16):
        out_ref[x] = dot(split(out_ref[x]), y)


def first_high_kernel(slab_ref, up_ref, above_ref, zo_ref, zh_ref, ah_ref, *refs):
    sum_ref, low_ref, halo_hbm, sems = refs
    copies = save_observed([above_ref], halo_hbm, sems)

    def obs(i, x):
        return (up_ref, above_ref)[i - 2][x, 64:, :]

    high_planes(slab_ref, up_ref, above_ref, obs, (zo_ref, zh_ref, ah_ref), sum_ref, low_ref)
    for copy in copies:
        copy.wait()


def first_low_kernel(slab_ref, low_ref, sum_ref, down_ref, below_ref, zl_ref, al_ref, ya_ref, *refs):
    out_ref, halo_hbm, sems = refs
    copies = save_observed([below_ref], halo_hbm, sems)

    def obs(i, x):
        return (below_ref, down_ref)[i][x, 64:, :]

    low_planes(slab_ref, low_ref, sum_ref, below_ref, obs, (zl_ref, al_ref, ya_ref), out_ref)
    for copy in copies:
        copy.wait()


def high_kernel(
    slab_ref, v_ref, above_ref, halo_ref, obs_ref, zo_ref, zh_ref, ah_ref, sum_ref, low_ref
):
    def obs(i, x):
        return obs_ref[x, 32:, :] if i == 2 else halo_ref[x]

    high_planes(slab_ref, v_ref, above_ref, obs, (zo_ref, zh_ref, ah_ref), sum_ref, low_ref)


def low_kernel(
    slab_ref, low_ref, sum_ref, below_ref, obs_ref, halo_ref, zl_ref, al_ref, ya_ref,
    out_ref, back_ref, rows_ref
):
    def obs(i, x):
        return obs_ref[x, :32, :] if i else halo_ref[x]

    low_planes(slab_ref, low_ref, sum_ref, below_ref, obs, (zl_ref, al_ref, ya_ref), back_ref)
    pack_one(back_ref, out_ref, rows_ref, 16, 0)


def per_device(observed, estimate, psf_y, psf_x, psf_z):
    core = lax.axis_index("c").reshape(1)
    slab = lax.axis_index("z").reshape(1)
    est0, obs0 = estimate.reshape(128, 1024), observed.reshape(128, 1024)

    first = pl.pallas_call(
        first_kernel,
        out_shape=pltpu.VMEM((2048, 128), jnp.float32),
        in_specs=[HBM, HBM, HBM],
        out_specs=VMEM,
        scratch_shapes=[
            pltpu.VMEM((128, 1024), jnp.float32),
            pltpu.VMEM((128, 1024), jnp.float32),
            pltpu.SMEM((31,), jnp.float32),
            pltpu.SemaphoreType.DMA((17,)),
        ],
        compiler_params=pltpu.CompilerParams(vmem_limit_bytes=LIMIT),
        name="first",
    )(*[pltpu.with_memory_space_constraint(a, pltpu.HBM) for a in (psf_x, est0, obs0)])
    arrived = exchange(first)
    yf, ya, xn, xf, zo, zl, zh, al, ah = prepare(psf_y, psf_x, psf_z)
    low_mats, high_mats = [zl, al, ya], [zo, zh, ah]
    halo = (16, 32, 128)
    out = [(16, 96, 128), (16, 96, 128)]
    up, down = call(arrive_kernel, out, [arrived, yf], 2, "arrive", [ROWS, ROWS, BLOCK])
    below = lax.ppermute(up, "z", UP)
    above = lax.ppermute(down, "z", DOWN)
    turned, obs = call(turn_kernel, ROWS, [est0, down, up], 1, "turn", save=BLOCK)
    rode = exchange(turned)
    args = [slab, up, above, *high_mats]
    total, low, halo_above = call(
        first_high_kernel, [BLOCK, BLOCK], args, 1, "first_high", save=halo
    )
    args = [slab, low, total, down, below, *low_mats]
    back, halo_below = call(first_low_kernel, BLOCK, args, 100, "first_low", save=halo)
    est = pl.pallas_call(
        unpack_kernel,
        out_shape=pltpu.VMEM(BLOCK, jnp.float32),
        in_specs=[HBM],
        out_specs=VMEM,
        scratch_shapes=[
            pltpu.VMEM(ROWS, jnp.float32),
            pltpu.VMEM(ROWS, jnp.float32),
            pltpu.SemaphoreType.DMA(()),
        ],
        cost_estimate=pl.CostEstimate(flops=10**9, bytes_accessed=10**6, transcendentals=0),
        compiler_params=pltpu.CompilerParams(vmem_limit_bytes=LIMIT),
        name="unpack",
    )(pltpu.with_memory_space_constraint(rode, pltpu.HBM))
    part = call(functools.partial(own_x_kernel, True), BLOCK, [psf_x, back], 1.3, "x_own")
    sides = [*x_halo(back), part]
    est_rows, v = call(
        functools.partial(update_kernel, True),
        [ROWS, BLOCK],
        [psf_x, core, *sides, est, yf],
        2,
        "update",
        [BLOCK, ROWS],
    )
    args = [psf_x, core, *x_halo(v), v]
    est_rows = exchange(est_rows)
    v = call(functools.partial(x_kernel, False), BLOCK, args, 100, "x_all")

    below = lax.ppermute(v, "z", UP)
    above = lax.ppermute(v, "z", DOWN)
    args = [slab, v, above, halo_above, obs, *high_mats]
    total, low = call(high_kernel, [BLOCK, BLOCK], args, 1, "ratio_high")
    args = [slab, low, total, below, obs, halo_below, *low_mats]
    rows = call(low_kernel, ROWS, args, 4, "ratio_low", [BLOCK, ROWS])
    rows = exchange(rows)
    out = pl.pallas_call(
        last_kernel,
        out_shape=pltpu.HBM((128, 1024), jnp.float32),
        in_specs=[VMEM] * 4,
        out_specs=HBM,
        scratch_shapes=[pltpu.VMEM((128, 1024), jnp.float32), pltpu.SemaphoreType.DMA((8,))],
        compiler_params=pltpu.CompilerParams(vmem_limit_bytes=LIMIT),
        name="last",
    )(*[pltpu.with_memory_space_constraint(a, pltpu.VMEM) for a in (rows, est_rows, xn, xf)])
    return out.reshape(8, 16, 1024)


def solution(mesh):
    fine = Mesh(mesh.devices.reshape(8, 4, 2, 4, 2), ("z", "x", "yl", "yh", "c"))
    spec = P(("z", "x", "yl"), ("yh", "c"), None)
    return jax.shard_map(
        per_device,
        mesh=fine,
        in_specs=(spec, spec, P(), P(), P()),
        out_specs=spec,
        check_vma=False,
    )
```

```python
import functools

import jax
import jax.numpy as jnp
from jax import lax
from jax.experimental import pallas as pl
from jax.experimental.pallas import tpu as pltpu
from jax.sharding import Mesh, PartitionSpec as P

LIMIT = 6 * 2**20
SLAB = ("x", "yl", "yh", "c")
BLOCK = (16, 64, 128)
ROWS = (1024, 128)
VMEM = pl.BlockSpec(memory_space=pltpu.VMEM)
SMEM = pl.BlockSpec(memory_space=pltpu.SMEM)
HBM = pl.BlockSpec(memory_space=pltpu.HBM)


def x_index(b, c):
    x, yh, yl = b // 8, (b % 8) // 2, b % 2
    return ((x * 2 + yl) * 4 + yh) * 2 + c


SWAP = [(0, 1), (1, 0)]
NEXT = [(x_index(b, 0), x_index(b - 1, 1)) for b in range(1, 32)] + [
    (x_index(b, 1), x_index(b + 1, 0)) for b in range(31)
]
UP = [(z, z + 1) for z in range(7)]
DOWN = [(z + 1, z) for z in range(7)]


def is_shape(s):
    return isinstance(s, tuple)


def call(kernel, out, args, us, name, scratch=(), save=None):
    args = [a if a.ndim == 1 else pltpu.with_memory_space_constraint(a, pltpu.VMEM) for a in args]
    shapes = jax.tree.map(lambda s: pltpu.VMEM(s, jnp.float32), out, is_leaf=is_shape)
    specs = jax.tree.map(lambda s: VMEM, out, is_leaf=is_shape)
    scratch = [pltpu.VMEM(s, jnp.float32) for s in scratch]
    if save:
        shapes = [*(shapes if isinstance(shapes, list) else [shapes]), pltpu.HBM(save, jnp.float32)]
        specs = [*(specs if isinstance(specs, list) else [specs]), HBM]
        scratch.append(pltpu.SemaphoreType.DMA((2,)))
    return pl.pallas_call(
        kernel,
        out_shape=shapes,
        in_specs=[SMEM if a.ndim == 1 else VMEM for a in args],
        out_specs=specs,
        scratch_shapes=scratch,
        cost_estimate=pl.CostEstimate(
            flops=int(us * 1e9), bytes_accessed=int(us * 3e6), transcendentals=0
        ),
        compiler_params=pltpu.CompilerParams(vmem_limit_bytes=LIMIT),
        name=name,
    )(*args)


def split(m):
    high = m.astype(jnp.bfloat16)
    return high, (m - high.astype(jnp.float32)).astype(jnp.bfloat16)


def dot(a, b):
    (ah, al), (bh, bl) = a, b

    def one(p, q):
        return jnp.dot(p, q, preferred_element_type=jnp.float32)

    return one(ah, bh) + (one(al, bh) + one(ah, bl))


def band(psf_ref, lead, flip, rows):
    taps = psf_ref.shape[0]
    lane = lax.broadcasted_iota(jnp.int32, (8, 256), 1)
    line = jnp.zeros((8, 256), jnp.float32)
    total = psf_ref[0]
    for k in range(taps):
        if k:
            total = total + psf_ref[k]
        line = jnp.where(lane == (k + lead) % 256, psf_ref[taps - 1 - k if flip else k], line)
    line = line / jnp.full((8, 256), total, jnp.float32)
    return pltpu.roll(jnp.broadcast_to(line[:1], (rows, 256)), 0, 1, stride=1, stride_axis=0)


def x_band(psf_ref, flip):
    m = band(psf_ref, -15, not flip, 128)
    return m[:, :128], m[:, 128:]


def prep_kernel(
    psf_y_ref, psf_x_ref, psf_z_ref, yf_ref, ya_ref, xn_ref, xf_ref, zo_ref, zl_ref, zh_ref, al_ref, ah_ref
):
    yf_ref[...] = band(psf_y_ref, -15, True, 128)[:, :128]
    ya_ref[...] = band(psf_y_ref, -15, False, 128)[:, :128]
    xn_ref[...], xf_ref[...] = x_band(psf_x_ref, True)
    fwd = band(psf_z_ref, 1, False, 128)
    zl_ref[...] = fwd[:64, :64]
    zo_ref[...] = fwd[:, 64:128]
    zh_ref[...] = fwd[64:, 128:192]
    adjoint = band(psf_z_ref, 1, True, 64)
    al_ref[...], ah_ref[...] = adjoint[:, :64], adjoint[:, 64:128]


def prepare(psf_y, psf_x, psf_z):
    out = [(128, 128)] * 4 + [(128, 64)] + [(64, 64)] * 4
    return call(prep_kernel, out, [psf_y, psf_x, psf_z], 1, "prepare")


def blur_lanes(tiles, near, far):
    lane = lax.broadcasted_iota(jnp.int32, tiles[0].shape, 1)
    zero = jnp.zeros_like(tiles[0])
    near, far = split(near), split(far)
    out = []
    for t in range(8):
        after = tiles[t + 1] if t < 7 else zero
        before = tiles[t - 1] if t > 0 else zero
        out.append(dot(split(tiles[t]), near) + dot(split(jnp.where(lane < 64, after, before)), far))
    return out


def rows_at(t, i, per=16, offset=0):
    block = 8 * t + i
    return x_index(block // 2, block % 2) * per + offset


def write_columns(out_ref, t, tile, per=16, offset=0):
    turned = tile.T
    for i in range(8):
        at = rows_at(t, i, per, offset)
        out_ref[at : at + 16, :] = turned[16 * i : 16 * i + 16, :]


def first_kernel(psf_x_hbm, est_hbm, obs_hbm, out_ref, est_ref, obs_ref, psf_x_ref, sems):
    taps = pltpu.make_async_copy(psf_x_hbm, psf_x_ref, sems.at[16])
    taps.start()
    copies = [
        pltpu.make_async_copy(
            src.at[pl.ds(64 * i, 64), :], dst.at[pl.ds(64 * i, 64), :], sems.at[2 * n + i]
        )
        for n, (src, dst) in enumerate(((est_hbm, est_ref), (obs_hbm, obs_ref)))
        for i in range(2)
    ]
    for copy in copies:
        copy.start()
    taps.wait()
    near, far = x_band(psf_x_ref, False)
    copies[0].wait()
    copies[1].wait()
    blurred = blur_lanes([est_ref[:, 128 * t : 128 * t + 128] for t in range(8)], near, far)
    for t in range(8):
        write_columns(out_ref, t, blurred[t], 32, 0)
    copies[2].wait()
    copies[3].wait()
    for t in range(8):
        write_columns(out_ref, t, obs_ref[:, 128 * t : 128 * t + 128], 32, 16)


def save_observed(refs, out_hbm, sems):
    copies = [
        pltpu.make_async_copy(
            ref.at[:, pl.ds(64, 32), :], out_hbm.at[:, pl.ds(32 * i, 32), :], sems.at[i]
        )
        for i, ref in enumerate(refs)
    ]
    for copy in copies:
        copy.start()
    return copies


def turn_kernel(in_ref, down_ref, up_ref, out_ref, obs_hbm, sems):
    copies = save_observed([down_ref, up_ref], obs_hbm, sems)
    for t in range(8):
        write_columns(out_ref, t, in_ref[:, 128 * t : 128 * t + 128])
    for copy in copies:
        copy.wait()


def last_kernel(back_ref, est_ref, near_ref, far_ref, out_hbm, out_ref, sems):
    def tile(ref, t):
        spots = [rows_at(t, i) for i in range(8)]
        return jnp.concatenate([ref[at : at + 16, :] for at in spots], axis=0).T

    blurred = blur_lanes([tile(back_ref, t) for t in range(8)], near_ref[...], far_ref[...])
    copies = []
    for t in range(8):
        spot = pl.ds(128 * t, 128)
        out_ref[:, spot] = blurred[t] * tile(est_ref, t)
        copies.append(pltpu.make_async_copy(out_ref.at[:, spot], out_hbm.at[:, spot], sems.at[t]))
        copies[t].start()
    for copy in copies:
        copy.wait()


def swap_groups(tiles):
    group = lax.broadcasted_iota(jnp.int32, (8, 128), 1) // 16
    tiles = [tiles[0]] + [pltpu.roll(tiles[i], 16 * i, 1) for i in range(1, 8)]
    for b in (1, 2, 4):
        taken = (group & b) != 0
        tiles = [jnp.where(taken, tiles[(i + b) % 8], tiles[i]) for i in range(8)]
    return [tiles[0]] + [pltpu.roll(tiles[8 - i], 128 - 16 * i, 1) for i in range(1, 8)]


def unpack_one(in_ref, place, rows_ref, per, offset):
    for zc in range(8):
        for half in range(2):
            at = zc * 8 * per + half * 8 + offset
            tiles = swap_groups([in_ref[at + per * i : at + per * i + 8, :] for i in range(8)])
            at = zc * 128 + half * 8
            for i in range(8):
                rows_ref[at + 16 * i : at + 16 * i + 8, :] = tiles[i]
    for zc in range(8):
        for x in range(16):
            out_ref, at = place(zc * 8)
            out_ref[x, at : at + 8, :] = rows_ref[pl.ds(zc * 128 + x, 8, stride=16), :]


def unpack_kernel(in_hbm, out_ref, in_ref, rows_ref, sem):
    copy = pltpu.make_async_copy(in_hbm, in_ref, sem)
    copy.start()
    copy.wait()
    unpack_one(in_ref, lambda z: (out_ref, z), rows_ref, 16, 0)


def arrive_kernel(in_ref, y_ref, up_ref, down_ref, rows_ref, more_ref, v_ref):
    unpack_one(in_ref, lambda z: (v_ref, z), rows_ref, 32, 0)
    unpack_one(in_ref, lambda z: (up_ref, z + 32) if z >= 32 else (down_ref, z + 64), more_ref, 32, 16)
    y = split(y_ref[...])
    for x in range(16):
        v = dot(split(v_ref[x]), y)
        up_ref[x, :64, :] = v
        down_ref[x, :64, :] = v


def pack_one(in_ref, out_ref, rows_ref, per, offset):
    for zc in range(8):
        for x in range(16):
            rows_ref[pl.ds(zc * 128 + x, 8, stride=16), :] = in_ref[x, zc * 8 : zc * 8 + 8, :]
    for zc in range(8):
        for half in range(2):
            at = zc * 128 + half * 8
            tiles = swap_groups([rows_ref[at + 16 * i : at + 16 * i + 8, :] for i in range(8)])
            at = zc * 8 * per + half * 8 + offset
            for i in range(8):
                out_ref[at + per * i : at + per * i + 8, :] = tiles[i]


def exchange(rows):
    per = rows.shape[0] // 64
    t = lax.all_to_all(rows.reshape(64, per, 128), SLAB, 0, 0, tiled=True)
    return t.reshape(rows.shape)


def tap_vectors(psf_ref, flip):
    total = psf_ref[0]
    for k in range(1, 31):
        total = total + psf_ref[k]
    scale = 1.0 / jnp.full((8, 128), total, jnp.float32)
    return [psf_ref[30 - k if flip else k] * scale for k in range(31)]


def add_block(w, ref, z, acc, shift):
    for j in range(16):
        v = ref[j, z, :]
        for i in range(16):
            k = j + shift - i + 15
            if 0 <= k <= 30:
                p = w[k] * v
                acc[i] = p if acc[i] is None else acc[i] + p
    return acc


def over_planes(body):
    def step(t, _):
        body(pl.ds(pl.multiple_of(t * 8, 8), 8))
        return 0

    lax.fori_loop(0, 8, step, 0)


def own_x_kernel(flip, psf_ref, own_ref, out_ref):
    w = tap_vectors(psf_ref, flip)

    def body(z):
        acc = add_block(w, own_ref, z, [None] * 16, 0)
        for i in range(16):
            out_ref[i, z, :] = acc[i]

    over_planes(body)


def add_sides(w, core_ref, start, passed_ref, swapped_ref, finish):
    def run(shift):
        def body(z):
            acc = start(z)
            acc = add_block(w, swapped_ref, z, acc, shift)
            finish(z, add_block(w, passed_ref, z, acc, -shift))

        over_planes(body)

    pl.when(core_ref[0] == 0)(lambda: run(16))
    pl.when(core_ref[0] != 0)(lambda: run(-16))


def x_kernel(flip, psf_ref, core_ref, swapped_ref, passed_ref, own_ref, out_ref):
    w = tap_vectors(psf_ref, flip)

    def start(z):
        return add_block(w, own_ref, z, [None] * 16, 0)

    def finish(z, acc):
        for i in range(16):
            out_ref[i, z, :] = acc[i]

    add_sides(w, core_ref, start, passed_ref, swapped_ref, finish)


def update_kernel(
    flip, psf_ref, core_ref, swapped_ref, passed_ref, part_ref, est_ref, y_ref, rows_ref, out_ref,
    new_ref, turn_ref
):
    def finish(z, acc):
        for i in range(16):
            new_ref[i, z, :] = est_ref[i, z, :] * acc[i]

    def start(z):
        return [part_ref[i, z, :] for i in range(16)]

    w = tap_vectors(psf_ref, flip)
    add_sides(w, core_ref, start, passed_ref, swapped_ref, finish)
    y = split(y_ref[...])
    for i in range(16):
        out_ref[i] = dot(split(new_ref[i]), y)
    pack_one(new_ref, rows_ref, turn_ref, 16, 0)


def x_halo(v):
    swapped = lax.ppermute(v, "c", SWAP)
    passed = lax.ppermute(v, SLAB, NEXT)
    return [swapped, passed]


def high_planes(slab_ref, v_ref, above_ref, obs, mats, sum_ref, low_ref):
    has_above = jnp.full((32, 128), slab_ref[0], jnp.int32) < 7
    own, band, adjoint = [split(m[...]) for m in mats]
    for x in range(16):
        part = dot(own, split(v_ref[x, :64, :]))
        low_ref[x] = part[:64]
        sum_ref[x] = part[64:] + dot(band, split(above_ref[x, :64, :]))
    for x in range(16):
        sum_ref[x, :32, :] = obs(2, x) / sum_ref[x, :32, :]
        sum_ref[x, 32:, :] = jnp.where(has_above, obs(3, x) / sum_ref[x, 32:, :], 0.0)
    for x in range(16):
        sum_ref[x] = dot(adjoint, split(sum_ref[x]))


def low_planes(slab_ref, low_ref, sum_ref, below_ref, obs, mats, out_ref):
    has_below = jnp.full((32, 128), slab_ref[0], jnp.int32) > 0
    band, adjoint, y = [split(m[...]) for m in mats]
    for x in range(16):
        out_ref[x] = low_ref[x] + dot(band, split(below_ref[x, :64, :]))
    for x in range(16):
        out_ref[x, :32, :] = jnp.where(has_below, obs(0, x) / out_ref[x, :32, :], 0.0)
        out_ref[x, 32:, :] = obs(1, x) / out_ref[x, 32:, :]
    for x in range(16):
        out_ref[x] = sum_ref[x] + dot(adjoint, split(out_ref[x]))
    for x in range(16):
        out_ref[x] = dot(split(out_ref[x]), y)


def first_high_kernel(slab_ref, up_ref, above_ref, zo_ref, zh_ref, ah_ref, *refs):
    sum_ref, low_ref, halo_hbm, sems = refs
    copies = save_observed([above_ref], halo_hbm, sems)

    def obs(i, x):
        return (up_ref, above_ref)[i - 2][x, 64:, :]

    high_planes(slab_ref, up_ref, above_ref, obs, (zo_ref, zh_ref, ah_ref), sum_ref, low_ref)
    for copy in copies:
        copy.wait()


def first_low_kernel(slab_ref, low_ref, sum_ref, down_ref, below_ref, zl_ref, al_ref, ya_ref, *refs):
    out_ref, halo_hbm, sems = refs
    copies = save_observed([below_ref], halo_hbm, sems)

    def obs(i, x):
        return (below_ref, down_ref)[i][x, 64:, :]

    low_planes(slab_ref, low_ref, sum_ref, below_ref, obs, (zl_ref, al_ref, ya_ref), out_ref)
    for copy in copies:
        copy.wait()


def high_kernel(
    slab_ref, v_ref, above_ref, halo_ref, obs_ref, zo_ref, zh_ref, ah_ref, sum_ref, low_ref
):
    def obs(i, x):
        return obs_ref[x, 32:, :] if i == 2 else halo_ref[x]

    high_planes(slab_ref, v_ref, above_ref, obs, (zo_ref, zh_ref, ah_ref), sum_ref, low_ref)


def low_kernel(
    slab_ref, low_ref, sum_ref, below_ref, obs_ref, halo_ref, zl_ref, al_ref, ya_ref,
    out_ref, back_ref, rows_ref
):
    def obs(i, x):
        return obs_ref[x, :32, :] if i else halo_ref[x]

    low_planes(slab_ref, low_ref, sum_ref, below_ref, obs, (zl_ref, al_ref, ya_ref), back_ref)
    pack_one(back_ref, out_ref, rows_ref, 16, 0)


def per_device(observed, estimate, psf_y, psf_x, psf_z):
    core = lax.axis_index("c").reshape(1)
    slab = lax.axis_index("z").reshape(1)
    est0, obs0 = estimate.reshape(128, 1024), observed.reshape(128, 1024)

    first = pl.pallas_call(
        first_kernel,
        out_shape=pltpu.VMEM((2048, 128), jnp.float32),
        in_specs=[HBM, HBM, HBM],
        out_specs=VMEM,
        scratch_shapes=[
            pltpu.VMEM((128, 1024), jnp.float32),
            pltpu.VMEM((128, 1024), jnp.float32),
            pltpu.SMEM((31,), jnp.float32),
            pltpu.SemaphoreType.DMA((17,)),
        ],
        compiler_params=pltpu.CompilerParams(vmem_limit_bytes=LIMIT),
        name="first",
    )(*[pltpu.with_memory_space_constraint(a, pltpu.HBM) for a in (psf_x, est0, obs0)])
    arrived = exchange(first)
    yf, ya, xn, xf, zo, zl, zh, al, ah = prepare(psf_y, psf_x, psf_z)
    low_mats, high_mats = [zl, al, ya], [zo, zh, ah]
    halo = (16, 32, 128)
    out = [(16, 96, 128), (16, 96, 128)]
    up, down = call(arrive_kernel, out, [arrived, yf], 2, "arrive", [ROWS, ROWS, BLOCK])
    below = lax.ppermute(up, "z", UP)
    above = lax.ppermute(down, "z", DOWN)
    turned, obs = call(turn_kernel, ROWS, [est0, down, up], 1, "turn", save=BLOCK)
    rode = exchange(turned)
    args = [slab, up, above, *high_mats]
    total, low, halo_above = call(
        first_high_kernel, [BLOCK, BLOCK], args, 1, "first_high", save=halo
    )
    args = [slab, low, total, down, below, *low_mats]
    back, halo_below = call(first_low_kernel, BLOCK, args, 100, "first_low", save=halo)
    est = pl.pallas_call(
        unpack_kernel,
        out_shape=pltpu.VMEM(BLOCK, jnp.float32),
        in_specs=[HBM],
        out_specs=VMEM,
        scratch_shapes=[
            pltpu.VMEM(ROWS, jnp.float32),
            pltpu.VMEM(ROWS, jnp.float32),
            pltpu.SemaphoreType.DMA(()),
        ],
        cost_estimate=pl.CostEstimate(flops=10**9, bytes_accessed=10**6, transcendentals=0),
        compiler_params=pltpu.CompilerParams(vmem_limit_bytes=LIMIT),
        name="unpack",
    )(pltpu.with_memory_space_constraint(rode, pltpu.HBM))
    part = call(functools.partial(own_x_kernel, True), BLOCK, [psf_x, back], 1.3, "x_own")
    sides = [*x_halo(back), part]
    est_rows, v = call(
        functools.partial(update_kernel, True),
        [ROWS, BLOCK],
        [psf_x, core, *sides, est, yf],
        2,
        "update",
        [BLOCK, ROWS],
    )
    args = [psf_x, core, *x_halo(v), v]
    est_rows = exchange(est_rows)
    v = call(functools.partial(x_kernel, False), BLOCK, args, 100, "x_all")

    below = lax.ppermute(v, "z", UP)
    above = lax.ppermute(v, "z", DOWN)
    args = [slab, v, above, halo_above, obs, *high_mats]
    total, low = call(high_kernel, [BLOCK, BLOCK], args, 1, "ratio_high")
    args = [slab, low, total, below, obs, halo_below, *low_mats]
    rows = call(low_kernel, ROWS, args, 4, "ratio_low", [BLOCK, ROWS])
    rows = exchange(rows)
    out = pl.pallas_call(
        last_kernel,
        out_shape=pltpu.HBM((128, 1024), jnp.float32),
        in_specs=[VMEM] * 4,
        out_specs=HBM,
        scratch_shapes=[pltpu.VMEM((128, 1024), jnp.float32), pltpu.SemaphoreType.DMA((8,))],
        compiler_params=pltpu.CompilerParams(vmem_limit_bytes=LIMIT),
        name="last",
    )(*[pltpu.with_memory_space_constraint(a, pltpu.VMEM) for a in (rows, est_rows, xn, xf)])
    return out.reshape(8, 16, 1024)


def solution(mesh):
    fine = Mesh(mesh.devices.reshape(8, 4, 2, 4, 2), ("z", "x", "yl", "yh", "c"))
    spec = P(("z", "x", "yl"), ("yh", "c"), None)
    return jax.shard_map(
        per_device,
        mesh=fine,
        in_specs=(spec, spec, P(), P(), P()),
        out_specs=spec,
        check_vma=False,
    )
```
